256 devices in a mesh: surf: 32 (over z, y_hi, core), neur: 8 (over x, y_lo).
Axes of the slice: x: 4, y: 4 (y_hi: 2, y_lo: 2; y = y_hi * 2 + y_lo), z: 8, core: 2. Of those that a mesh axis runs over, the one named last changes fastest.
Arguments:
- spike_bins: int32 [16, 64, 32768], P(None, 'neur', 'surf'), may hold values from 0 to 10
- neuron_site: int32 [64, 32768], P('neur', 'surf'), may hold values from 0 to 1023
- efficacy: bfloat16 [64, 32768], P('neur', 'surf'), may hold values from 0.5 to 2
- region_live: int32 [64], P('neur'), may hold values from 1 to 32768, 1258291 in all
- membrane_init: float32 [16, 64, 32768], P(None, 'neur', 'surf'), may hold values from -4 to 4
- field_init: float32 [16, 64, 1024], P(None, 'neur', 'surf'), may hold values from -6 to 6
- rim_weights: float32 [6, 64, 1024], P(None, 'neur', 'surf'), may hold values from 0.2 to 1
- rim_codes: int32 [6, 64, 1024], P(None, 'neur', 'surf'), may hold values from 0 to 24, as said below
Outputs:
- field_final: float32 [16, 64, 1024], P(None, 'neur', 'surf')
- membranes: float32 [16, 64, 32768], P(None, 'neur', 'surf')
The draws below stay inside these ranges and needn't reach their ends.
Inputs may be any that keep to these rules, and one draw needn't show every extreme that they name: `spike_bins`: a bin of 10 means that the neuron does not spike in the window. `rim_codes`: the codes of one vertex are distinct and never 2 * 6.
All inputs are finite; a program needn't handle non-finite values. No bound on the sum of `region_live` on one device may be relied on, other than what follows from the above.
Results may differ from the reference program's by a relative error of at most 0.006.
Values may be sent and summed in bfloat16 or wider, within the bound.
A program may use at most 256 MiB of HBM per device.

```python
import math
import jax
import jax.numpy as jnp
import numpy as np
from jax import lax

STEPS = 10
TRIALS = 16
NEUR_DEV = 1024
NEIGHBORS = 6
RIM = 2
FOOT = 8
REGIONS = 64
VR = 1024
NPR = 32768
N_SURF = 32


def draw_rim_codes(key, part):
    reach_span = 2 * RIM + 1
    others = reach_span * reach_span - 1
    scores = jax.random.randint(key, (REGIONS, VR, others), 0, 1 << 20)
    scores = scores * 64 + jnp.arange(others, dtype=jnp.int32)
    chosen = lax.top_k(scores, NEIGHBORS)[1].astype(jnp.int32)
    self_code = RIM * reach_span + RIM
    vertex_codes = chosen + (chosen >= self_code).astype(jnp.int32)
    return jnp.transpose(vertex_codes, (2, 0, 1))


def place_ends(drawn, own_key, smallest, top_value):
    shape = drawn.shape
    place = [jax.random.randint(jax.random.fold_in(own_key, axis), (), 0, shape[axis]) for axis in range(len(shape))]
    drawn = drawn.at[tuple(place)].set(smallest)
    longest = shape.index(max(shape))
    place[longest] = (place[longest] + 1) % shape[longest]
    return drawn.at[tuple(place)].set(top_value)


def steps_of(own_key, dims, cuts, least, top_value):
    gain = 1.0
    for position, parts in cuts:
        heights = jax.random.uniform(jax.random.fold_in(jax.random.fold_in(own_key, 6), position), (parts,), jnp.float32, least / len(cuts), top_value / len(cuts))
        gain = gain * jnp.repeat(jnp.exp(heights), dims[position] // parts).reshape((-1,) + (1,) * (len(dims) - 1 - position))
    return gain


def split_up(number_of, total, most, lean):
    loads = [(1 << 20) // math.isqrt(rank ** lean) + 1 for rank in range(2, number_of + 1)]
    rest, counts = total - most - (number_of - 1), [1] * (number_of - 1)
    while rest > 0:
        free = [i for i in range(number_of - 1) if counts[i] < most]
        pool, left = sum([loads[i] for i in free]), rest
        for i in free:
            addition = min(most - counts[i], max(1, left * loads[i] // pool), rest)
            counts[i] = counts[i] + addition
            rest = rest - addition
    return np.array([most] + counts)


def uneven_parts(key, number_of, total, reach, skew):
    if number_of == 2:
        one = jax.random.randint(key, (), max(1, total - reach), min(reach, total - 1) + 1)
        return jnp.stack([one, total - one])
    sizes = jnp.asarray(split_up(number_of, total, reach, skew), jnp.int32)
    couples = (number_of - 1) // 2
    giver, taker = sizes[1:1 + 2 * couples:2], sizes[2:2 + 2 * couples:2]
    slack = jnp.minimum(giver - 1, reach - taker)
    shifted = jax.random.randint(jax.random.fold_in(key, 1), (couples,), 0, 1 << 20) % (slack + 1)
    sizes = sizes.at[1:1 + 2 * couples:2].set(giver - shifted).at[2:2 + 2 * couples:2].set(taker + shifted)
    return sizes[jax.random.permutation(jax.random.fold_in(key, 2), number_of)]


def bell_draw(key, extent, width, limit, pieces=(), kind=jnp.bfloat16):
    array = jax.random.normal(key, extent, jnp.float32) * width
    if len(pieces) > 0:
        array = steps_of(key, extent, pieces, -0.22, 0.18) * array
    return jnp.clip(array, min=-limit, max=limit).astype(kind)


def setup_inputs(seed: int = 0) -> dict:
    streams_of = jax.random.split(jax.random.key(seed), 9)
    spike_bins = place_ends(jax.random.randint(streams_of[0], (TRIALS, REGIONS, NPR), 0, STEPS + 1), jax.random.fold_in(streams_of[0], 1), 0, STEPS).astype(jnp.int32)
    neuron_site = place_ends(jax.random.randint(streams_of[1], (REGIONS, NPR), 0, VR), jax.random.fold_in(streams_of[1], 1), 0, VR - 1).astype(jnp.int32)
    efficacy = jnp.clip(jnp.exp(math.log(2.0) - 1.3862944 * jax.random.uniform(streams_of[2], (REGIONS, NPR), jnp.float32) ** steps_of(streams_of[2], (REGIONS, NPR), ((0, 8), (1, 32)), -0.2, 0.2)), 0.5, 2.0).astype(jnp.bfloat16)
    region_live = uneven_parts(streams_of[3], REGIONS, REGIONS * NPR * 3 // 5, NPR, 2).astype(jnp.int32)
    membrane_init = bell_draw(streams_of[4], (TRIALS, REGIONS, NPR), 0.5, 4.0, ((1, 8), (2, 32)), jnp.float32)
    field_init = bell_draw(streams_of[5], (TRIALS, REGIONS, VR), 1.0, 6.0, ((1, 8), (2, 32)), jnp.float32)
    rim_weights = jnp.clip(0.2 + 0.8 * jax.random.uniform(streams_of[6], (NEIGHBORS, REGIONS, VR), jnp.float32) ** steps_of(streams_of[6], (NEIGHBORS, REGIONS, VR), ((1, 8), (2, 32)), -0.2, 0.2), 0.2, 1.0)
    rim_codes = draw_rim_codes(jax.random.fold_in(streams_of[8], 71), 0)
    return {"spike_bins": spike_bins, "neuron_site": neuron_site, "efficacy": efficacy, "region_live": region_live, "membrane_init": membrane_init, "field_init": field_init, "rim_weights": rim_weights, "rim_codes": rim_codes}


def footprint():
    spread = jnp.exp(-0.5 * jnp.arange(FOOT, dtype=jnp.float32))
    return spread / jnp.sum(spread)


def stencil(rim_weights, rim_codes):
    reach_span = 2 * RIM + 1
    entries = []
    for row_shift in range(-RIM, RIM + 1):
        for col_shift in range(-RIM, RIM + 1):
            if row_shift == 0 and col_shift == 0:
                continue
            code_value = (row_shift + RIM) * reach_span + (col_shift + RIM)
            weight = jnp.sum(jnp.where(rim_codes == code_value, rim_weights, jnp.zeros_like(rim_weights)), axis=0)
            entries.append((row_shift, col_shift, weight))
    return entries, jnp.sum(rim_weights, axis=0)


def reference(spike_bins, neuron_site, efficacy, region_live, membrane_init, field_init, rim_weights, rim_codes):
    kernel = footprint()
    slot_ids = jnp.arange(NPR, dtype=jnp.int32)
    is_live = slot_ids[None, :] < region_live[:, None]
    times = jnp.arange(STEPS, dtype=jnp.int32)
    bins_by_region = jnp.transpose(spike_bins, (1, 0, 2))

    def region_rates(inputs):
        bins_region, sites_region, weights_region, live_region = inputs
        bins_moved = jnp.transpose(bins_region)
        elapsed = (times[None, :, None] - bins_moved[:, None, :]).astype(jnp.float32)
        has_fired = (bins_moved[:, None, :] <= times[None, :, None]) & live_region[:, None, None]
        values = jnp.where(has_fired, weights_region.astype(jnp.float32)[:, None, None] * jnp.exp(-0.35 * elapsed), jnp.zeros_like(elapsed))
        rounded_charge = lax.optimization_barrier(values.astype(jnp.bfloat16))
        charge_rows = rounded_charge.astype(jnp.float32).reshape(NPR, STEPS * TRIALS)
        shard_ids = slot_ids // NEUR_DEV
        totals = jnp.zeros((N_SURF * VR, STEPS * TRIALS), jnp.float32)
        for offset in range(FOOT):
            target = shard_ids * VR + (sites_region + offset) % VR
            totals = totals + jax.ops.segment_sum(charge_rows * kernel[offset], target, num_segments=N_SURF * VR)
        rounded = lax.optimization_barrier(totals.astype(jnp.bfloat16)).astype(jnp.float32)
        return jnp.sum(rounded.reshape(N_SURF, VR, STEPS * TRIALS), axis=0)

    rate_table = lax.map(region_rates, (bins_by_region, neuron_site, efficacy, is_live))
    rate_steps = jnp.transpose(rate_table.reshape(REGIONS, VR, STEPS, TRIALS), (2, 3, 0, 1))
    entries, weight_sum = stencil(rim_weights, rim_codes)

    def field_step(field_now, rate_now):
        wide_field = jnp.concatenate([field_now[:, :, VR - RIM:], field_now, field_now[:, :, :RIM]], axis=2)
        full_field = jnp.pad(wide_field, ((0, 0), (RIM, RIM), (0, 0)))
        spread_sum = -weight_sum * field_now
        for row_shift, col_shift, weight in entries:
            spread_sum = spread_sum + weight * full_field[:, RIM + row_shift:RIM + row_shift + REGIONS, RIM + col_shift:RIM + col_shift + VR]
        field_next = 0.9 * field_now + 0.15 * spread_sum + 0.1 * rate_now
        return field_next, field_next.astype(jnp.bfloat16)

    field_final, history = lax.scan(field_step, field_init, rate_steps)
    history_by_region = jnp.transpose(history, (2, 0, 1, 3))
    membrane_by_region = jnp.transpose(membrane_init, (1, 0, 2))

    def region_cells(inputs):
        bins_region, sites_region, history_region, start_region, live_region = inputs
        neuron_drive = jnp.zeros((STEPS, TRIALS, NPR), jnp.float32)
        for offset in range(FOOT):
            target = (sites_region + offset) % VR
            neuron_drive = neuron_drive + history_region[:, :, target].astype(jnp.float32) * kernel[offset]
        voltage = start_region
        for step_index in range(STEPS):
            voltage = 0.9 * voltage + 0.5 * neuron_drive[step_index]
            voltage = jnp.where(bins_region == step_index, -0.5 * jnp.ones_like(voltage), voltage)
        return jnp.where(live_region[None, :], voltage, jnp.zeros_like(voltage))

    cells = lax.map(region_cells, (bins_by_region, neuron_site, history_by_region, membrane_by_region, is_live))
    membranes = jnp.transpose(cells, (1, 0, 2))
    return field_final, membranes
```

```python
import math

import jax
import jax.numpy as jnp
from jax import lax
from jax.experimental import pallas as pl
from jax.experimental.pallas import tpu as pltpu
from jax.sharding import PartitionSpec as P

STEPS = 10
RIM = 2
FOOT = 8
TAPS = (0.84375, 0.51171875, 0.310546875, 0.1884765625, 0.1142578125, 0.0693359375, 0.0419921875, 0.025390625)
SCALE = 1.0 / sum(TAPS)
DECAY = math.exp(-0.35)
F32 = jnp.float32
BF16 = jnp.bfloat16
VMEM_LIMIT = 56 * 1024 * 1024
ROWS = 80
LANES = 128


def build_band(site, band_ref):
    total, slots = band_ref.shape
    tiles = total // 16
    high = jnp.broadcast_to((site >> 4).astype(F32).astype(BF16), (16, slots))
    low = jnp.broadcast_to(site & 15, (16, slots))
    row = lax.broadcasted_iota(jnp.int32, (16, slots), 0)
    first = jnp.zeros((16, slots), F32)
    second = jnp.zeros((16, slots), F32)
    for offset in range(FOOT):
        first = jnp.where(row - low == offset, TAPS[offset], first)
        second = jnp.where(row + 16 - low == offset, TAPS[offset], second)
    first, second = first.astype(BF16), second.astype(BF16)
    zero = jnp.zeros((16, slots), BF16)
    for tile in range(tiles):
        here = high == jnp.asarray(tile, BF16)
        before = high == jnp.asarray((tile - 1) % tiles, BF16)
        band_ref[tile * 16 : tile * 16 + 16, :] = jnp.where(here, first, jnp.where(before, second, zero))


def spread_kernel(live_ref, bins_ref, site_ref, eff_ref, out_ref, band_ref):
    region = pl.program_id(0)
    slots = site_ref.shape[1]
    slot = lax.axis_index("surf") * slots + lax.broadcasted_iota(jnp.int32, (1, slots), 1)
    weight = jnp.where(slot < live_ref[region], eff_ref[pl.ds(region, 1), :], 0.0)
    weight = jnp.broadcast_to(weight, (8, slots))
    build_band(site_ref[pl.ds(region, 1), :], band_ref)
    rows = []
    for half in range(2):
        bins = bins_ref[half, :, 0, 0]
        for step in range(STEPS):
            rows.append(jnp.where(bins == step, weight, 0.0))
    charge = jnp.concatenate(rows, axis=0).astype(BF16)
    total = lax.dot_general(charge, band_ref[...], (((1,), (1,)), ((), ())), preferred_element_type=F32)
    total = (total * SCALE).astype(BF16)
    for plane in range(8):
        for half in range(2):
            out_ref[plane, half, 0] = total[half * ROWS : half * ROWS + ROWS, plane * LANES : plane * LANES + LANES]


def collect_kernel(live_ref, gather_ref, bins_ref, site_ref, init_ref, out_ref, band_ref):
    region = pl.program_id(0)
    slots = site_ref.shape[1]
    slot = lax.axis_index("surf") * slots + lax.broadcasted_iota(jnp.int32, (8, slots), 1)
    live = slot < live_ref[region]
    build_band(site_ref[pl.ds(region, 1), :], band_ref)
    history = jnp.concatenate(
        [jnp.concatenate([gather_ref[plane, 0, 0], gather_ref[plane, 1, 0]], axis=0) for plane in range(8)], axis=1
    )
    drive = jnp.dot(history, band_ref[...], preferred_element_type=F32)
    for half in range(2):
        bins = bins_ref[half, :, 0, 0]
        voltage = init_ref[half, :, 0, 0]
        for step in range(STEPS):
            start = half * ROWS + step * 8
            voltage = 0.9 * voltage + (0.5 * SCALE) * drive[start : start + 8]
            voltage = jnp.where(bins == step, -0.5, voltage)
        out_ref[half, :, 0, 0] = jnp.where(live, voltage, 0.0)


def field_kernel(
    s_ref, rim_ref, init_ref, g_ref, ff_ref,
    cx_ref, sbuf, rbuf, rq_ref, iq_ref, tl_ref, til_ref, ro_ref, rh_ref, io_ref, ih_ref, p_ref, mb_ref,
    own_ref, hal_ref, inj_ref, cf_ref, hist_ref, mb2_ref, h2_ref, t_ref, ffs_ref, ffr_ref,
    cx_send, cx_recv, ring_send, ring_recv, q_send, q_recv, r2_send, r2_recv, a_send, a_recv,
    b_send, b_recv, f_send, f_recv, ag_send, ag_recv, ac_send, ac_recv,
):
    s = lax.axis_index("surf")
    g = lax.axis_index("neur")
    z = s // 4
    yh = (s // 2) % 2
    c = s % 2
    dzh = 2 * yh - 1

    def dev(zz, yy, cc, gg):
        return {"surf": lax.rem(zz + 16, 8) * 4 + yy * 2 + cc, "neur": gg}

    def rdma(src, dst, ss, rs, target):
        return pltpu.make_async_remote_copy(
            src_ref=src, dst_ref=dst, send_sem=ss, recv_sem=rs, device_id=target, device_id_type=pl.DeviceIdType.MESH
        )

    def zmod(dz):
        return lax.rem(z + dz + 16, 8)

    def gmod(i):
        return lax.rem(g + i, 8)

    barrier = pltpu.get_barrier_semaphore()
    me = (yh * 2 + c) * 8 + g

    def greet_plane(i, carry):
        other = lax.rem(me + i, 32)
        pl.semaphore_signal(
            barrier, inc=1, device_id=dev(z, other // 16, (other // 8) % 2, other % 8), device_id_type=pl.DeviceIdType.MESH
        )
        return carry

    lax.fori_loop(1, 32, greet_plane, 0)

    def greet_near(i, carry):
        pl.semaphore_signal(
            barrier, inc=1, device_id=dev(z + dzh, i // 8, c, i % 8), device_id_type=pl.DeviceIdType.MESH
        )
        return carry

    lax.fori_loop(0, 16, greet_near, 0)
    pl.semaphore_signal(barrier, inc=1, device_id=dev(z - dzh, yh, c, g), device_id_type=pl.DeviceIdType.MESH)
    pl.semaphore_wait(barrier, 31 + 17)

    partner = dev(z, yh, 1 - c, g)
    order = (4, 3, 5, 2, 6, 1, 7, 0)
    cx = {}
    for dz in order:
        cx[dz] = rdma(s_ref.at[zmod(dz), 1 - c], cx_ref.at[zmod(dz)], cx_send.at[dz], cx_recv.at[dz], partner)
        cx[dz].start()

    q = yh * 2 + c
    quad = []
    for i in range(1, 4):
        y2 = lax.rem(yh + i // 2, 2)
        c2 = lax.rem(c + i % 2, 2)
        target = dev(z, y2, c2, g)
        quad.append((y2 * 2 + c2, rdma(rim_ref, rq_ref.at[q], q_send.at[i], q_recv.at[q], target)))
        quad.append((y2 * 2 + c2, rdma(init_ref.at[pl.ds(c2 * 8, 8)], iq_ref.at[q], q_send.at[4 + i], q_recv.at[4 + q], target)))
    for _, copy in quad:
        copy.start()
    rq_ref[q] = rim_ref[...]
    iq_ref[q] = init_ref[pl.ds(c * 8, 8)]

    def x_of(dz, half):
        zd = zmod(dz)
        return s_ref[zd, c, half * 4 : half * 4 + 4].astype(F32) + cx_ref[zd, half * 4 : half * 4 + 4].astype(F32)

    ring = {}

    def ring_step(slot):
        letter, k = slot
        for way, sign in ((0, 1), (1, -1)):
            half = way if letter == "A" else 1 - way
            dz = sign * (4 - k)
            index = k if letter == "A" else 3 + k
            value = x_of(dz, half)
            first = k == (0 if letter == "A" else 1)
            if not first:
                ring[(way, index - 1)].wait_recv()
                value = value + rbuf[way, index - 1].astype(F32)
            sbuf[way, index] = value.astype(BF16)
            copy = rdma(
                sbuf.at[way, index], rbuf.at[way, index], ring_send.at[way, index], ring_recv.at[way, index],
                dev(z + sign, yh, c, g),
            )
            copy.start()
            ring[(way, index)] = copy

    cx[4].wait_recv()
    ring_step(("A", 0))
    cx[3].wait_recv()
    cx[5].wait_recv()
    ring_step(("B", 1))

    lane = lax.broadcasted_iota(jnp.int32, (8, LANES), 1)
    for i in range(1, 4):
        y2 = lax.rem(yh + i // 2, 2)
        c2 = lax.rem(c + i % 2, 2)
        src = y2 * 2 + c2
        rdma(rim_ref, rq_ref.at[src], q_send.at[i], q_recv.at[src], partner).wait_recv()
        rdma(init_ref.at[pl.ds(0, 8)], iq_ref.at[src], q_send.at[4 + i], q_recv.at[4 + src], partner).wait_recv()
    block = lane // 32
    for k in range(12):
        tl_ref[k] = jnp.where(
            block < 2,
            jnp.where(block == 0, rq_ref[0, k], rq_ref[1, k]),
            jnp.where(block == 2, rq_ref[2, k], rq_ref[3, k]),
        )
    for k in range(8):
        til_ref[k] = jnp.where(
            block < 2,
            jnp.where(block == 0, iq_ref[0, k], iq_ref[1, k]),
            jnp.where(block == 2, iq_ref[2, k], iq_ref[3, k]),
        )

    def setup_own(i):
        gg = gmod(i)
        target = dev(z, yh, c, gg)
        return (
            rdma(tl_ref, ro_ref.at[g], r2_send.at[0, i], r2_recv.at[0, g], target),
            rdma(til_ref.at[gg], io_ref.at[g], r2_send.at[1, i], r2_recv.at[1, g], target),
        )

    def setup_near(i):
        gg = gmod(i)
        target = dev(z - dzh, yh, c, gg)
        return (
            rdma(tl_ref, rh_ref.at[g], r2_send.at[2, i], r2_recv.at[2, g], target),
            rdma(til_ref.at[gg], ih_ref.at[g], r2_send.at[3, i], r2_recv.at[3, g], target),
        )

    def start_all(make):
        def body(i, carry):
            for copy in make(i):
                copy.start()
            return carry

        return body

    def sent_all(make):
        def body(i, carry):
            for copy in make(i):
                copy.wait_send()
            return carry

        return body

    lax.fori_loop(1, 8, start_all(setup_own), 0)
    lax.fori_loop(0, 8, start_all(setup_near), 0)
    ro_ref[g] = tl_ref[...]
    io_ref[g] = til_ref[g]

    cx[2].wait_recv()
    cx[6].wait_recv()
    ring_step(("A", 1))
    ring_step(("B", 2))
    ring_step(("A", 2))
    cx[1].wait_recv()
    cx[7].wait_recv()
    cx[0].wait_recv()
    ring_step(("B", 3))

    def setup_arrived(i, carry):
        gg = gmod(i)

        @pl.when(i > 0)
        def _():
            rdma(tl_ref, ro_ref.at[gg], r2_send.at[0, i], r2_recv.at[0, gg], partner).wait_recv()
            rdma(til_ref.at[0], io_ref.at[gg], r2_send.at[1, i], r2_recv.at[1, gg], partner).wait_recv()

        rdma(tl_ref, rh_ref.at[gg], r2_send.at[2, i], r2_recv.at[2, gg], partner).wait_recv()
        rdma(til_ref.at[0], ih_ref.at[gg], r2_send.at[3, i], r2_recv.at[3, gg], partner).wait_recv()
        return carry

    lax.fori_loop(0, 8, setup_arrived, 0)
    mine = (lane >= 32 * yh) & (lane < 96 + 32 * yh)
    row8 = lax.broadcasted_iota(jnp.int32, (8, LANES), 0)

    def couple(gg, carry):
        weights = [jnp.where(mine, ro_ref[gg, k], rh_ref[gg, k]) for k in range(6)]
        codes = [jnp.where(mine, ro_ref[gg, 6 + k], rh_ref[gg, 6 + k]) for k in range(6)]
        rows = pl.ds(pl.multiple_of(gg * 8, 8), 8)
        region = gg * 8 + row8
        for a in range(-RIM, RIM + 1):
            inside = (region + a >= 0) & (region + a < 64)
            for b in range(-RIM, RIM + 1):
                code = (a + RIM) * (2 * RIM + 1) + b + RIM
                if a == 0 and b == 0:
                    cf_ref[code, rows] = 0.9 - 0.15 * (weights[0] + weights[1] + weights[2] + weights[3] + weights[4] + weights[5])
                    continue
                total = jnp.zeros((8, LANES), F32)
                for k in range(6):
                    total = total + jnp.where(codes[k] == float(code), weights[k], 0.0)
                cf_ref[code, rows] = jnp.where(inside, 0.15 * total, 0.0)
        ffs_ref[rows] = jnp.where(mine, io_ref[gg], ih_ref[gg])
        return carry

    lax.fori_loop(0, 8, couple, 0)
    for a in range(-RIM, RIM + 1):
        if a != 0:
            for b in range(2 * RIM + 1):
                code = (a + RIM) * (2 * RIM + 1) + b
                cf_ref[code] = pltpu.roll(cf_ref[code], a % 64, 0)

    ring_step(("A", 3))

    for half in range(2):
        value = x_of(0, half)
        for way in range(2):
            index = 3 if way == half else 6
            ring[(way, index)].wait_recv()
            value = value + rbuf[way, index].astype(F32)
        p_ref[half * 320 : half * 320 + 320, :] = value.reshape(320, LANES)

    for n in range(8):
        for pair in range(STEPS // 2):
            parts = [p_ref[pl.ds((2 * pair + j) * 8 + n, 8, stride=ROWS), :] for j in range(2)]
            mb_ref[n, pair * 16 : pair * 16 + 16] = jnp.concatenate(parts, axis=0).astype(BF16)
    slot = yh * 8 + g

    def trial_own(k):
        n = gmod(k % 8)
        return (rdma(mb_ref.at[n], own_ref.at[slot], a_send.at[0, k], a_recv.at[0, slot], dev(z, lax.rem(yh + k // 8, 2), c, n)),)

    def trial_near(k):
        n = gmod(k % 8)
        up = k // 8
        return (rdma(mb_ref.at[n], hal_ref.at[slot], a_send.at[1, k], a_recv.at[1, slot], dev(z + 1 - 2 * up, up, c, n)),)

    lax.fori_loop(1, 16, start_all(trial_own), 0)
    lax.fori_loop(0, 16, start_all(trial_near), 0)
    own_ref[slot] = mb_ref[g]

    def trial_arrived(k, carry):
        @pl.when(k != slot)
        def _():
            rdma(mb_ref.at[0], own_ref.at[k], a_send.at[0, 0], a_recv.at[0, k], partner).wait_recv()

        rdma(mb_ref.at[0], hal_ref.at[k], a_send.at[1, 0], a_recv.at[1, k], partner).wait_recv()
        return carry

    lax.fori_loop(0, 16, trial_arrived, 0)
    lane16 = lax.broadcasted_iota(jnp.int32, (16, LANES), 1)
    mine16 = (lane16 >= 32 * yh) & (lane16 < 96 + 32 * yh)

    def unpack(gg, carry):
        rows = pl.ds(pl.multiple_of(gg * 8, 8), 8)
        for pair in range(STEPS // 2):
            tile = slice(pair * 16, pair * 16 + 16)
            value = jnp.where(
                mine16,
                own_ref[gg, tile].astype(F32) + own_ref[8 + gg, tile].astype(F32),
                hal_ref[gg, tile].astype(F32) + hal_ref[8 + gg, tile].astype(F32),
            )
            inj_ref[2 * pair, rows] = value[:8]
            inj_ref[2 * pair + 1, rows] = value[8:]
        return carry

    lax.fori_loop(0, 8, unpack, 0)

    def advance(step, carry):
        field, rate = carry
        rate = DECAY * rate + inj_ref[step]
        total = 0.1 * rate
        shifted = [field if b == 0 else pltpu.roll(field, (-b) % LANES, 1) for b in range(-RIM, RIM + 1)]
        for a in range(-RIM, RIM + 1):
            term = None
            for b in range(2 * RIM + 1):
                product = cf_ref[(a + RIM) * (2 * RIM + 1) + b] * shifted[b]
                term = product if term is None else term + product
            total = total + (term if a == 0 else pltpu.roll(term, (-a) % 64, 0))
        hist_ref[step] = total
        return (total, rate)

    last, _ = lax.fori_loop(0, STEPS, advance, (ffs_ref[...], jnp.zeros((64, LANES), F32)))
    ffs_ref[...] = last

    def pack(gg, carry):
        rows = pl.ds(pl.multiple_of(gg * 8, 8), 8)
        for pair in range(STEPS // 2):
            mb2_ref[gg, pair * 16 : pair * 16 + 16] = jnp.concatenate(
                [hist_ref[2 * pair, rows], hist_ref[2 * pair + 1, rows]], axis=0
            ).astype(BF16)
        return carry

    lax.fori_loop(0, 8, pack, 0)

    def back(k):
        gg = gmod(k % 8)
        return (rdma(mb2_ref.at[gg], h2_ref.at[slot], b_send.at[k], b_recv.at[slot], dev(z, lax.rem(yh + k // 8, 2), c, gg)),)

    trial = c * 8 + g

    def final(k):
        gg = gmod(k % 8)
        rows = pl.ds(pl.multiple_of(gg * 8, 8), 8)
        return (rdma(ffs_ref.at[rows], ffr_ref.at[trial], f_send.at[k], f_recv.at[trial], dev(z, yh, lax.rem(c + k // 8, 2), gg)),)

    lax.fori_loop(1, 16, start_all(back), 0)
    lax.fori_loop(1, 16, start_all(final), 0)
    h2_ref[slot] = mb2_ref[g]
    ffr_ref[trial] = ffs_ref[pl.ds(pl.multiple_of(g * 8, 8), 8)]

    def back_arrived(k, carry):
        @pl.when(k != slot)
        def _():
            rdma(mb2_ref.at[0], h2_ref.at[k], b_send.at[0], b_recv.at[k], partner).wait_recv()

        return carry

    lax.fori_loop(0, 16, back_arrived, 0)
    for n in range(8):
        for pair in range(STEPS // 2):
            tile = slice(pair * 16, pair * 16 + 16)
            value = jnp.where(lane16 < 64, h2_ref[n, tile].astype(F32), h2_ref[8 + n, tile].astype(F32))
            t_ref[pl.ds(pair * 128 + n, 16, stride=8), :] = value
    for r in range(8):
        for pair in range(STEPS // 2):
            parts = [t_ref[(2 * pair + j) * 64 + r * 8 : (2 * pair + j) * 64 + r * 8 + 8, :] for j in range(2)]
            g_ref[z, c, r, pair * 16 : pair * 16 + 16] = jnp.concatenate(parts, axis=0).astype(BF16)

    ag = {}
    pieces = []

    def to_core(zz, half, index):
        piece = g_ref.at[zz, c, pl.ds(half * 4, 4)]
        copy = rdma(piece, piece, ac_send.at[index], ac_recv.at[index], partner)
        copy.start()
        pieces.append((zz, half, index, copy))

    def ag_step(slot_index, letter, k):
        for way, sign in ((0, 1), (1, -1)):
            half = way if letter == 0 else 1 - way
            zz = zmod(-sign * k)
            if k > 0:
                ag[(way, slot_index - 2)].wait_recv()
            piece = g_ref.at[zz, c, pl.ds(half * 4, 4)]
            copy = rdma(piece, piece, ag_send.at[way, slot_index], ag_recv.at[way, slot_index], dev(z + sign, yh, c, g))
            copy.start()
            ag[(way, slot_index)] = copy
            if k > 0:
                to_core(zz, half, way * 7 + slot_index - 2)

    for slot_index in range(7):
        ag_step(slot_index, slot_index % 2, slot_index // 2)
        if slot_index == 1:
            to_core(z, 0, 14)
            to_core(z, 1, 15)

    def final_arrived(k, carry):
        @pl.when(k != trial)
        def _():
            rdma(ffs_ref.at[pl.ds(0, 8)], ffr_ref.at[k], f_send.at[0], f_recv.at[k], partner).wait_recv()

        return carry

    lax.fori_loop(0, 16, final_arrived, 0)
    for k in range(16):
        value = pltpu.roll(ffr_ref[k], lax.rem(128 - 32 * q, 128), 1)
        ff_ref[k] = value[:, :32]

    for slot_index in (5, 6):
        for way, sign in ((0, 1), (1, -1)):
            ag[(way, slot_index)].wait_recv()
            letter, k = slot_index % 2, slot_index // 2
            half = way if letter == 0 else 1 - way
            to_core(zmod(-sign * (k + 1)), half, way * 7 + slot_index)
    for zz, half, index, copy in pieces:
        other = g_ref.at[zz, 1 - c, pl.ds(half * 4, 4)]
        rdma(other, other, ac_send.at[index], ac_recv.at[index], partner).wait_recv()

    for dz in order:
        cx[dz].wait_send()
    for _, copy in quad:
        copy.wait_send()
    for copy in ring.values():
        copy.wait_send()
    lax.fori_loop(1, 8, sent_all(setup_own), 0)
    lax.fori_loop(0, 8, sent_all(setup_near), 0)
    lax.fori_loop(1, 16, sent_all(trial_own), 0)
    lax.fori_loop(0, 16, sent_all(trial_near), 0)
    lax.fori_loop(1, 16, sent_all(back), 0)
    lax.fori_loop(1, 16, sent_all(final), 0)
    for copy in ag.values():
        copy.wait_send()
    for _, _, _, copy in pieces:
        copy.wait_send()


def local(spike_bins, neuron_site, efficacy, region_live, membrane_init, field_init, rim_weights, rim_codes):
    trials, regions, slots = spike_bins.shape
    bins5 = spike_bins.reshape(2, 8, regions, 1, slots)
    init5 = membrane_init.reshape(2, 8, regions, 1, slots)
    smem = pl.BlockSpec(memory_space=pltpu.SMEM)
    vmem = pl.BlockSpec(memory_space=pltpu.VMEM)
    row_block = pl.BlockSpec((2, 8, 1, 1, slots), lambda r: (0, 0, r, 0, 0))
    whole = pl.BlockSpec((regions, slots), lambda r: (0, 0))
    field_block = pl.BlockSpec((8, 2, 1, ROWS, LANES), lambda r: (0, 0, r, 0, 0))
    params = pltpu.CompilerParams(vmem_limit_bytes=VMEM_LIMIT)
    spread = pl.pallas_call(
        spread_kernel,
        grid=(regions,),
        out_shape=jax.ShapeDtypeStruct((8, 2, regions, ROWS, LANES), BF16),
        in_specs=[smem, row_block, whole, whole],
        out_specs=field_block,
        scratch_shapes=[pltpu.VMEM((1024, slots), BF16)],
        compiler_params=params,
        name="spread",
    )(region_live, bins5, neuron_site, efficacy.astype(F32))
    rim = jnp.tile(jnp.concatenate([rim_weights, rim_codes.astype(F32)], axis=0), (1, 1, 4))
    init = jnp.tile(field_init, (1, 1, 4))
    dma = pltpu.SemaphoreType.DMA
    gathered, field_final = pl.pallas_call(
        field_kernel,
        out_shape=(
            jax.ShapeDtypeStruct((8, 2, regions, ROWS, LANES), BF16),
            jax.ShapeDtypeStruct((16, 8, 32), F32),
        ),
        in_specs=[vmem, vmem, vmem],
        out_specs=(vmem, vmem),
        scratch_shapes=[
            pltpu.VMEM((8, 8, ROWS, LANES), BF16),
            pltpu.VMEM((2, 7, 4, ROWS, LANES), BF16),
            pltpu.VMEM((2, 7, 4, ROWS, LANES), BF16),
            pltpu.VMEM((4, 12, 8, LANES), F32),
            pltpu.VMEM((4, 8, 8, LANES), F32),
            pltpu.VMEM((12, 8, LANES), F32),
            pltpu.VMEM((8, 8, LANES), F32),
            pltpu.VMEM((8, 12, 8, LANES), F32),
            pltpu.VMEM((8, 12, 8, LANES), F32),
            pltpu.VMEM((8, 8, LANES), F32),
            pltpu.VMEM((8, 8, LANES), F32),
            pltpu.VMEM((640, LANES), F32),
            pltpu.VMEM((8, ROWS, LANES), BF16),
            pltpu.VMEM((16, ROWS, LANES), BF16),
            pltpu.VMEM((16, ROWS, LANES), BF16),
            pltpu.VMEM((STEPS, 64, LANES), F32),
            pltpu.VMEM((25, 64, LANES), F32),
            pltpu.VMEM((STEPS, 64, LANES), F32),
            pltpu.VMEM((8, ROWS, LANES), BF16),
            pltpu.VMEM((16, ROWS, LANES), BF16),
            pltpu.VMEM((640, LANES), F32),
            pltpu.VMEM((64, LANES), F32),
            pltpu.VMEM((16, 8, LANES), F32),
            dma((8,)), dma((8,)), dma((2, 7)), dma((2, 7)), dma((8,)), dma((8,)),
            dma((4, 8)), dma((4, 8)), dma((2, 16)), dma((2, 16)), dma((16,)), dma((16,)),
            dma((16,)), dma((16,)), dma((2, 7)), dma((2, 7)), dma((16,)), dma((16,)),
        ],
        compiler_params=pltpu.CompilerParams(vmem_limit_bytes=VMEM_LIMIT, collective_id=0, has_side_effects=True),
        name="field",
    )(spread, rim, init)
    membranes = pl.pallas_call(
        collect_kernel,
        grid=(regions,),
        out_shape=jax.ShapeDtypeStruct((2, 8, regions, 1, slots), F32),
        in_specs=[smem, field_block, row_block, whole, row_block],
        out_specs=row_block,
        scratch_shapes=[pltpu.VMEM((1024, slots), BF16)],
        compiler_params=params,
        name="collect",
    )(region_live, gathered, bins5, neuron_site, init5)
    return field_final, membranes.reshape(trials, regions, slots)


def solution(mesh):
    in_specs = (
        P(None, "neur", "surf"),
        P("neur", "surf"),
        P("neur", "surf"),
        P("neur"),
        P(None, "neur", "surf"),
        P(None, "neur", "surf"),
        P(None, "neur", "surf"),
        P(None, "neur", "surf"),
    )
    out_specs = (P(None, "neur", "surf"), P(None, "neur", "surf"))
    return jax.shard_map(local, mesh=mesh, in_specs=in_specs, out_specs=out_specs, check_vma=False)
```

```python
import math

import jax
import jax.numpy as jnp
from jax import lax
from jax.experimental import pallas as pl
from jax.experimental.pallas import tpu as pltpu
from jax.sharding import PartitionSpec as P

STEPS = 10
RIM = 2
FOOT = 8
TAPS = (0.84375, 0.51171875, 0.310546875, 0.1884765625, 0.1142578125, 0.0693359375, 0.0419921875, 0.025390625)
SCALE = 1.0 / sum(TAPS)
DECAY = math.exp(-0.35)
F32 = jnp.float32
BF16 = jnp.bfloat16
VMEM_LIMIT = 56 * 1024 * 1024
ROWS = 80
LANES = 128


def build_band(site, band_ref):
    total, slots = band_ref.shape[-2:]
    tiles = total // 16
    high = jnp.broadcast_to((site >> 4).astype(F32).astype(BF16), (16, slots))
    low = jnp.broadcast_to(site & 15, (16, slots))
    row = lax.broadcasted_iota(jnp.int32, (16, slots), 0)
    first = jnp.zeros((16, slots), F32)
    second = jnp.zeros((16, slots), F32)
    for offset in range(FOOT):
        first = jnp.where(row - low == offset, TAPS[offset], first)
        second = jnp.where(row + 16 - low == offset, TAPS[offset], second)
    first, second = first.astype(BF16), second.astype(BF16)
    zero = jnp.zeros((16, slots), BF16)
    for tile in range(tiles):
        here = high == jnp.asarray(tile, BF16)
        before = high == jnp.asarray((tile - 1) % tiles, BF16)
        band_ref[tile * 16 : tile * 16 + 16, :] = jnp.where(here, first, jnp.where(before, second, zero))


def fused_kernel(
    live_ref, bins_ref, site_ref, eff_ref, start_ref, field_ref, weights_ref, codes_ref,
    ff_ref, out_ref,
    weff_ref, tbins_ref, tstart_ref, band_ref, charge_ref, drive_ref, s_ref, g_ref, rim_ref, init_ref,
    cx_ref, sbuf, rbuf, rq_ref, iq_ref, tl_ref, til_ref, th_ref, tih_ref, tm_ref, tim_ref, ro_ref, io_ref, p_ref, mb_ref, mh_ref,
    own_ref, hal_ref, inj_ref, cf_ref, hist_ref, mb2_ref, h2_ref, t_ref, ffs_ref, ffr_ref,
    cx_send, cx_recv, ring_send, ring_recv, q_send, q_recv, n_send, n_recv, r2_send, r2_recv, a_send, a_recv,
    b_send, b_recv, f_send, f_recv, ag_send, ag_recv, ay_send, ay_recv, ac_send, ac_recv,
):
    s = lax.axis_index("surf")
    g = lax.axis_index("neur")
    z = s // 4
    yh = (s // 2) % 2
    c = s % 2
    dzh = 2 * yh - 1

    def dev(zz, yy, cc, gg):
        return {"surf": lax.rem(zz + 16, 8) * 4 + yy * 2 + cc, "neur": gg}

    def rdma(src, dst, ss, rs, target):
        return pltpu.make_async_remote_copy(
            src_ref=src, dst_ref=dst, send_sem=ss, recv_sem=rs, device_id=target, device_id_type=pl.DeviceIdType.MESH
        )

    def zmod(dz):
        return lax.rem(z + dz + 16, 8)

    def gmod(i):
        return lax.rem(g + i, 8)

    barrier = pltpu.get_barrier_semaphore()
    me = (yh * 2 + c) * 8 + g

    def greet_plane(i, carry):
        other = lax.rem(me + i, 32)
        pl.semaphore_signal(
            barrier, inc=1, device_id=dev(z, other // 16, (other // 8) % 2, other % 8), device_id_type=pl.DeviceIdType.MESH
        )
        return carry

    lax.fori_loop(1, 32, greet_plane, 0)

    def greet_near(i, carry):
        pl.semaphore_signal(
            barrier, inc=1, device_id=dev(z + dzh, i // 8, c, i % 8), device_id_type=pl.DeviceIdType.MESH
        )
        return carry

    lax.fori_loop(0, 16, greet_near, 0)
    pl.semaphore_signal(barrier, inc=1, device_id=dev(z - dzh, yh, c, g), device_id_type=pl.DeviceIdType.MESH)

    slots = site_ref.shape[1]
    slot_id = s * slots + lax.broadcasted_iota(jnp.int32, (1, slots), 1)

    for tile in range(8):
        tbins_ref[tile * 128 : tile * 128 + 128, :] = bins_ref[:, tile * LANES : tile * LANES + LANES]
        tstart_ref[tile * 128 : tile * 128 + 128, :] = start_ref[:, tile * LANES : tile * LANES + LANES]

    weff_ref[...] = eff_ref[...].astype(F32)

    def trials_of(ref, half, region):
        first = half * 64 + region
        return jnp.concatenate([ref[pl.ds(tile * 128 + first, 8, stride=8), :] for tile in range(8)], axis=1)

    def spread(region, carry):
        weight = jnp.where(slot_id < live_ref[region], weff_ref[pl.ds(region, 1), :], 0.0)
        weight = jnp.broadcast_to(weight, (8, slots))
        band = band_ref.at[region]
        build_band(site_ref[pl.ds(region, 1), :], band)
        for half in range(2):
            bins = trials_of(tbins_ref, half, region)
            for pair in range(STEPS // 2):
                rows = [jnp.where(bins == 2 * pair + j, weight, 0.0) for j in range(2)]
                start = half * ROWS + pair * 16
                charge_ref[start : start + 16, :] = jnp.concatenate(rows, axis=0).astype(BF16)
        total = lax.dot_general(charge_ref[...], band[...], (((1,), (1,)), ((), ())), preferred_element_type=F32)
        total = (total * SCALE).astype(BF16)
        for plane in range(8):
            for half in range(2):
                s_ref[plane, half, region] = total[half * ROWS : half * ROWS + ROWS, plane * LANES : plane * LANES + LANES]
        return carry

    partner = dev(z, yh, 1 - c, g)
    cx = {}

    def quarter(index):
        lax.fori_loop(2 * index, 2 * index + 2, spread, 0)

    def to_partner(index):
        part = pl.ds(2 * index, 2)
        cx[index] = rdma(s_ref.at[:, 1 - c, part], cx_ref.at[:, part], cx_send.at[index], cx_recv.at[index], partner)
        cx[index].start()

    quarter(0)
    pl.semaphore_wait(barrier, 31 + 17)
    to_partner(0)

    q = yh * 2 + c
    for k in range(6):
        rim_ref[k] = jnp.concatenate([weights_ref[k]] * 4, axis=1)
        rim_ref[6 + k] = jnp.concatenate([codes_ref[k].astype(F32)] * 4, axis=1)
    for k in range(16):
        init_ref[k] = jnp.concatenate([field_ref[k]] * 4, axis=1)
    quad = []
    for i in range(1, 4):
        y2 = lax.rem(yh + i // 2, 2)
        c2 = lax.rem(c + i % 2, 2)
        target = dev(z, y2, c2, g)
        quad.append((y2 * 2 + c2, rdma(rim_ref, rq_ref.at[q], q_send.at[i], q_recv.at[q], target)))
        quad.append((y2 * 2 + c2, rdma(init_ref.at[pl.ds(c2 * 8, 8)], iq_ref.at[q], q_send.at[4 + i], q_recv.at[4 + q], target)))
    for _, copy in quad:
        copy.start()
    rq_ref[q] = rim_ref[...]
    iq_ref[q] = init_ref[pl.ds(c * 8, 8)]


    def x_of(dz, index):
        zd = zmod(dz)
        part = slice(2 * index, 2 * index + 2)
        return s_ref[zd, c, part].astype(F32) + cx_ref[zd, part].astype(F32)

    ring = {}

    def hop(index, k):
        for way, sign in ((0, 1), (1, -1)):
            first = 4 if way == index % 2 else 3
            if k >= first:
                continue
            value = x_of(sign * (first - k), index)
            if k == 0:
                pass
            else:
                ring[(way, index, k - 1)].wait_recv()
                value = value + rbuf[way, index, k - 1].astype(F32)
            sbuf[way, index, k] = value.astype(BF16)
            copy = rdma(
                sbuf.at[way, index, k], rbuf.at[way, index, k], ring_send.at[way, index, k], ring_recv.at[way, index, k],
                dev(z + sign, yh, c, g),
            )
            copy.start()
            ring[(way, index, k)] = copy

    quarter(1)
    to_partner(1)
    cx[0].wait_recv()
    hop(0, 0)
    quarter(2)
    to_partner(2)
    cx[1].wait_recv()
    hop(1, 0)
    hop(0, 1)
    quarter(3)
    to_partner(3)
    cx[2].wait_recv()
    hop(2, 0)
    hop(1, 1)
    hop(0, 2)

    lane = lax.broadcasted_iota(jnp.int32, (8, LANES), 1)
    for i in range(1, 4):
        y2 = lax.rem(yh + i // 2, 2)
        c2 = lax.rem(c + i % 2, 2)
        src = y2 * 2 + c2
        rdma(rim_ref, rq_ref.at[src], q_send.at[i], q_recv.at[src], partner).wait_recv()
        rdma(init_ref.at[pl.ds(0, 8)], iq_ref.at[src], q_send.at[4 + i], q_recv.at[4 + src], partner).wait_recv()
    block = lane // 32
    for k in range(12):
        tl_ref[k] = jnp.where(
            block < 2,
            jnp.where(block == 0, rq_ref[0, k], rq_ref[1, k]),
            jnp.where(block == 2, rq_ref[2, k], rq_ref[3, k]),
        )
    for k in range(8):
        til_ref[k] = jnp.where(
            block < 2,
            jnp.where(block == 0, iq_ref[0, k], iq_ref[1, k]),
            jnp.where(block == 2, iq_ref[2, k], iq_ref[3, k]),
        )

    near = (
        rdma(tl_ref, th_ref, n_send.at[0], n_recv.at[0], dev(z - dzh, yh, c, g)),
        rdma(til_ref, tih_ref, n_send.at[1], n_recv.at[1], dev(z - dzh, yh, c, g)),
    )
    for copy in near:
        copy.start()

    def setup_own(i):
        gg = gmod(i)
        target = dev(z, yh, c, gg)
        return (
            rdma(tm_ref, ro_ref.at[g], r2_send.at[0, i], r2_recv.at[0, g], target),
            rdma(tim_ref.at[gg], io_ref.at[g], r2_send.at[1, i], r2_recv.at[1, g], target),
        )

    def start_all(make):
        def body(i, carry):
            for copy in make(i):
                copy.start()
            return carry

        return body

    def sent_all(make):
        def body(i, carry):
            for copy in make(i):
                copy.wait_send()
            return carry

        return body

    cx[3].wait_recv()
    hop(3, 0)
    hop(2, 1)
    hop(1, 2)

    mine = (lane >= 32 * yh) & (lane < 96 + 32 * yh)
    for copy in near:
        copy.wait_recv()
    for k in range(12):
        tm_ref[k] = jnp.where(mine, tl_ref[k], th_ref[k])
    for k in range(8):
        tim_ref[k] = jnp.where(mine, til_ref[k], tih_ref[k])
    lax.fori_loop(1, 8, start_all(setup_own), 0)
    ro_ref[g] = tm_ref[...]
    io_ref[g] = tim_ref[g]

    hop(0, 3)
    hop(3, 1)
    hop(2, 2)

    def setup_arrived(i, carry):
        gg = gmod(i)
        rdma(tm_ref, ro_ref.at[gg], r2_send.at[0, i], r2_recv.at[0, gg], partner).wait_recv()
        rdma(tim_ref.at[0], io_ref.at[gg], r2_send.at[1, i], r2_recv.at[1, gg], partner).wait_recv()
        return carry

    lax.fori_loop(1, 8, setup_arrived, 0)
    row8 = lax.broadcasted_iota(jnp.int32, (8, LANES), 0)

    def couple(gg, carry):
        weights = [ro_ref[gg, k] for k in range(6)]
        codes = [ro_ref[gg, 6 + k] for k in range(6)]
        rows = pl.ds(pl.multiple_of(gg * 8, 8), 8)
        region = gg * 8 + row8
        for a in range(-RIM, RIM + 1):
            inside = (region + a >= 0) & (region + a < 64)
            for b in range(-RIM, RIM + 1):
                code = (a + RIM) * (2 * RIM + 1) + b + RIM
                if a == 0 and b == 0:
                    cf_ref[code, rows] = 0.9 - 0.15 * (weights[0] + weights[1] + weights[2] + weights[3] + weights[4] + weights[5])
                    continue
                total = jnp.zeros((8, LANES), F32)
                for k in range(6):
                    total = total + jnp.where(codes[k] == float(code), weights[k], 0.0)
                cf_ref[code, rows] = jnp.where(inside, 0.15 * total, 0.0)
        ffs_ref[rows] = io_ref[gg]
        return carry

    lax.fori_loop(0, 8, couple, 0)
    for a in range(-RIM, RIM + 1):
        if a != 0:
            for b in range(2 * RIM + 1):
                code = (a + RIM) * (2 * RIM + 1) + b
                cf_ref[code] = pltpu.roll(cf_ref[code], a % 64, 0)

    hop(1, 3)
    hop(3, 2)
    hop(2, 3)
    hop(3, 3)

    for index in range(4):
        value = x_of(0, index)
        for way in range(2):
            k = 3 if way == index % 2 else 2
            ring[(way, index, k)].wait_recv()
            value = value + rbuf[way, index, k].astype(F32)
        p_ref[index * 160 : index * 160 + 160, :] = value.reshape(160, LANES)

    lane16 = lax.broadcasted_iota(jnp.int32, (16, LANES), 1)
    block16 = lane16 // 32

    def by_block(tiles):
        return jnp.where(
            block16 < 2, jnp.where(block16 == 0, tiles[0], tiles[1]), jnp.where(block16 == 2, tiles[2], tiles[3])
        )

    for n in range(8):
        tiles = []
        for pair in range(STEPS // 2):
            parts = [p_ref[pl.ds((2 * pair + j) * 8 + n, 8, stride=ROWS), :] for j in range(2)]
            tiles.append(jnp.concatenate(parts, axis=0))
            mb_ref[n, pair * 16 : pair * 16 + 16] = tiles[-1].astype(BF16)
        high = [pltpu.roll(tiles[j], 32 * j + 32, 1) if j < 3 else tiles[j] for j in range(4)]
        low = [pltpu.roll(tiles[j], 32 * j, 1) if j > 0 else tiles[j] for j in range(4)]
        mh_ref[0, n, :16] = by_block(high).astype(BF16)
        mh_ref[1, n, :16] = by_block(low).astype(BF16)
        mh_ref[0, n, 16:] = tiles[4].astype(BF16)
        mh_ref[1, n, 16:] = tiles[4].astype(BF16)
    slot = yh * 8 + g

    def trial_own(k):
        n = gmod(k % 8)
        return (rdma(mb_ref.at[n], own_ref.at[slot], a_send.at[0, k], a_recv.at[0, slot], dev(z, lax.rem(yh + k // 8, 2), c, n)),)

    def trial_near(k):
        n = gmod(k % 8)
        up = k // 8
        return (rdma(mh_ref.at[up, n], hal_ref.at[slot], a_send.at[1, k], a_recv.at[1, slot], dev(z + 1 - 2 * up, up, c, n)),)

    lax.fori_loop(1, 16, start_all(trial_own), 0)
    lax.fori_loop(0, 16, start_all(trial_near), 0)
    own_ref[slot] = mb_ref[g]

    def trial_arrived(k, carry):
        @pl.when(k != slot)
        def _():
            rdma(mb_ref.at[0], own_ref.at[k], a_send.at[0, 0], a_recv.at[0, k], partner).wait_recv()

        rdma(mh_ref.at[0, 0], hal_ref.at[k], a_send.at[1, 0], a_recv.at[1, k], partner).wait_recv()
        return carry

    lax.fori_loop(0, 16, trial_arrived, 0)
    mine16 = (lane16 >= 32 * yh) & (lane16 < 96 + 32 * yh)

    def unpack(gg, carry):
        rows = pl.ds(pl.multiple_of(gg * 8, 8), 8)
        edge = hal_ref[gg].astype(F32) + hal_ref[8 + gg].astype(F32)
        for pair in range(STEPS // 2):
            tile = slice(pair * 16, pair * 16 + 16)
            near_edge = pltpu.roll(edge[:16], lax.rem(96 * (1 - yh) - 32 * pair + 128, 128), 1) if pair < 4 else edge[16:]
            value = jnp.where(mine16, own_ref[gg, tile].astype(F32) + own_ref[8 + gg, tile].astype(F32), near_edge)
            inj_ref[2 * pair, rows] = value[:8]
            inj_ref[2 * pair + 1, rows] = value[8:]
        return carry

    lax.fori_loop(0, 8, unpack, 0)

    def advance(step, carry):
        field, rate = carry
        rate = DECAY * rate + inj_ref[step]
        total = 0.1 * rate
        shifted = [field if b == 0 else pltpu.roll(field, (-b) % LANES, 1) for b in range(-RIM, RIM + 1)]
        for a in range(-RIM, RIM + 1):
            term = None
            for b in range(2 * RIM + 1):
                product = cf_ref[(a + RIM) * (2 * RIM + 1) + b] * shifted[b]
                term = product if term is None else term + product
            total = total + (term if a == 0 else pltpu.roll(term, (-a) % 64, 0))
        hist_ref[step] = total
        return (total, rate)

    last, _ = lax.fori_loop(0, STEPS, advance, (ffs_ref[...], jnp.zeros((64, LANES), F32)))
    ffs_ref[...] = last

    mine64 = (lane16 >= 64 * yh) & (lane16 < 64 + 64 * yh)

    def pack(gg, carry):
        rows = pl.ds(pl.multiple_of(gg * 8, 8), 8)
        tiles = [
            jnp.concatenate([hist_ref[2 * pair, rows], hist_ref[2 * pair + 1, rows]], axis=0) for pair in range(STEPS // 2)
        ]
        for m in range(2):
            both = jnp.where(mine64, tiles[2 * m], pltpu.roll(tiles[2 * m + 1], 64, 1))
            mb2_ref[gg, m * 16 : m * 16 + 16] = both.astype(BF16)
        mb2_ref[gg, 32:48] = tiles[4].astype(BF16)
        return carry

    lax.fori_loop(0, 8, pack, 0)

    def back(k):
        gg = gmod(k % 8)
        return (rdma(mb2_ref.at[gg], h2_ref.at[slot], b_send.at[k], b_recv.at[slot], dev(z, lax.rem(yh + k // 8, 2), c, gg)),)

    trial = c * 8 + g

    def final(k):
        gg = gmod(k % 8)
        rows = pl.ds(pl.multiple_of(gg * 8, 8), 8)
        return (rdma(ffs_ref.at[rows], ffr_ref.at[trial], f_send.at[k], f_recv.at[trial], dev(z, yh, lax.rem(c + k // 8, 2), gg)),)

    lax.fori_loop(1, 16, start_all(back), 0)
    lax.fori_loop(1, 16, start_all(final), 0)
    h2_ref[slot] = mb2_ref[g]
    ffr_ref[trial] = ffs_ref[pl.ds(pl.multiple_of(g * 8, 8), 8)]

    def back_arrived(k, carry):
        @pl.when(k != slot)
        def _():
            rdma(mb2_ref.at[0], h2_ref.at[k], b_send.at[0], b_recv.at[k], partner).wait_recv()

        return carry

    lax.fori_loop(0, 16, back_arrived, 0)
    for n in range(8):
        for m in range(3):
            tile = slice(m * 16, m * 16 + 16)
            left, right = h2_ref[n, tile].astype(F32), h2_ref[8 + n, tile].astype(F32)
            t_ref[pl.ds(2 * m * 128 + n, 16, stride=8), :] = jnp.where(lane16 < 64, left, right)
            if m < 2:
                t_ref[pl.ds((2 * m + 1) * 128 + n, 16, stride=8), :] = pltpu.roll(jnp.where(lane16 < 64, right, left), 64, 1)
    for r in range(8):
        for pair in range(STEPS // 2):
            parts = [t_ref[(2 * pair + j) * 64 + r * 8 : (2 * pair + j) * 64 + r * 8 + 8, :] for j in range(2)]
            g_ref[z, c, r, pair * 16 : pair * 16 + 16] = jnp.concatenate(parts, axis=0).astype(BF16)

    quarters = (yh, 2, 3)
    ag, ay, ac = {}, {}, []

    def piece(zz, half, index):
        return g_ref.at[zz, half, pl.ds(2 * index, 2)]

    def source(way, k):
        return zmod(-1 - k if way == 0 else 1 + k)

    def arrives(way, k, i):
        return k < 3 or (way == 0 and i < 2) or (way == 1 and i == 2)

    def pass_on(way, k, i):
        zz = z if k == 0 else source(way, k - 1)
        part = piece(zz, c, quarters[i])
        copy = rdma(part, part, ag_send.at[way, k, i], ag_recv.at[way, k, i], dev(z + 1 - 2 * way, yh, c, g))
        copy.start()
        ag[(way, k, i)] = copy

    def to_core(part, other, index, k):
        copy = rdma(part, part, ac_send.at[index], ac_recv.at[index], partner)
        copy.start()
        ac.append((copy, rdma(other, other, ac_send.at[index], ac_recv.at[index], partner), k))

    def arrived(way, k, i):
        ag[(way, k, i)].wait_recv()
        zz = source(way, k)
        part = piece(zz, c, quarters[i])
        if i == 0:
            other = piece(zz, c, 1 - yh)
            copy = rdma(part, part, ay_send.at[way, k], ay_recv.at[way, k], dev(z, 1 - yh, c, g))
            copy.start()
            ay[(way, k)] = (copy, rdma(other, other, ay_send.at[way, k], ay_recv.at[way, k], dev(z, 1 - yh, c, g)))
            if k == 3:
                copy = rdma(part, part, ay_send.at[1, 3], ay_recv.at[1, 3], dev(z, 1 - yh, 1 - c, g))
                copy.start()
                other = piece(zz, 1 - c, 1 - yh)
                ay[(1, 3)] = (copy, rdma(other, other, ay_send.at[1, 3], ay_recv.at[1, 3], partner))
        to_core(part, piece(zz, 1 - c, quarters[i]), (way * 4 + k) * 3 + i, k)

    def crossed(way, k):
        ay[(way, k)][1].wait_recv()
        zz = source(way, k)
        to_core(piece(zz, c, 1 - yh), piece(zz, 1 - c, 1 - yh), 24 + way * 4 + k, k)

    for i in range(3):
        for way in range(2):
            pass_on(way, 0, i)
    own_part, own_other = g_ref.at[z, c], g_ref.at[z, 1 - c]
    own_copy = rdma(own_part, own_part, ac_send.at[32], ac_recv.at[32], partner)
    own_copy.start()

    def final_arrived(k, carry):
        @pl.when(k != trial)
        def _():
            rdma(ffs_ref.at[pl.ds(0, 8)], ffr_ref.at[k], f_send.at[0], f_recv.at[k], partner).wait_recv()

        return carry

    lax.fori_loop(0, 16, final_arrived, 0)
    for k in range(16):
        value = pltpu.roll(ffr_ref[k], lax.rem(128 - 32 * q, 128), 1)
        ff_ref[k] = value[:, :32]

    for k in range(1, 4):
        for i in range(3):
            for way in range(2):
                if arrives(way, k, i):
                    arrived(way, k - 1, i)
                    pass_on(way, k, i)
        for i in range(3):
            for way in range(2):
                if not arrives(way, k, i):
                    arrived(way, k - 1, i)
        if k >= 2:
            for way in range(2):
                crossed(way, k - 2)

    near_planes = (z, zmod(1), zmod(-1), zmod(2), zmod(-2))
    far_planes = (zmod(3), zmod(-3), zmod(4))

    def product(region, planes):
        history = jnp.concatenate(
            [jnp.concatenate([g_ref[plane, 0, region], g_ref[plane, 1, region]], axis=0) for plane in planes], axis=1
        )
        band = jnp.concatenate(
            [band_ref[region, pl.ds(pl.multiple_of(plane * LANES, LANES), LANES), :] for plane in planes], axis=0
        )
        return jnp.dot(history, band, preferred_element_type=F32)

    def collect_near(region, carry):
        drive_ref[region] = product(region, near_planes)
        return carry

    rdma(own_other, own_other, ac_send.at[32], ac_recv.at[32], partner).wait_recv()
    for _, other, k in ac:
        if k < 2:
            other.wait_recv()
    lax.fori_loop(0, 4, collect_near, 0)
    crossed(0, 2)
    crossed(1, 2)
    for i in range(3):
        for way in range(2):
            if arrives(way, 3, i):
                arrived(way, 3, i)
    lax.fori_loop(4, 8, collect_near, 0)
    ay[(0, 3)][1].wait_recv()
    ay[(1, 3)][1].wait_recv()
    for _, other, k in ac:
        if k >= 2:
            other.wait_recv()

    slot8 = s * slots + lax.broadcasted_iota(jnp.int32, (8, slots), 1)

    def collect(region, carry):
        drive_ref[region] = drive_ref[region] + product(region, far_planes)
        live = slot8 < live_ref[region]
        for half in range(2):
            bins = trials_of(tbins_ref, half, region)
            voltage = trials_of(tstart_ref, half, region)
            for step in range(STEPS):
                start = half * ROWS + step * 8
                voltage = 0.9 * voltage + (0.5 * SCALE) * drive_ref[region, start : start + 8, :]
                voltage = jnp.where(bins == step, -0.5, voltage)
            voltage = jnp.where(live, voltage, 0.0)
            for tile in range(8):
                tstart_ref[pl.ds(tile * 128 + half * 64 + region, 8, stride=8), :] = voltage[:, tile * LANES : tile * LANES + LANES]
        return carry

    lax.fori_loop(0, 8, collect, 0)
    for tile in range(8):
        out_ref[:, tile * LANES : tile * LANES + LANES] = tstart_ref[tile * 128 : tile * 128 + 128, :]

    for copy in cx.values():
        copy.wait_send()
    for _, copy in quad:
        copy.wait_send()
    for copy in ring.values():
        copy.wait_send()
    lax.fori_loop(1, 8, sent_all(setup_own), 0)
    for copy in near:
        copy.wait_send()
    lax.fori_loop(1, 16, sent_all(trial_own), 0)
    lax.fori_loop(0, 16, sent_all(trial_near), 0)
    lax.fori_loop(1, 16, sent_all(back), 0)
    lax.fori_loop(1, 16, sent_all(final), 0)
    own_copy.wait_send()
    for copy in ag.values():
        copy.wait_send()
    for copy, _ in ay.values():
        copy.wait_send()
    for copy, _, _ in ac:
        copy.wait_send()


def local(spike_bins, neuron_site, efficacy, region_live, membrane_init, field_init, rim_weights, rim_codes):
    trials, regions, slots = spike_bins.shape
    rows = trials * regions
    vmem = pl.BlockSpec(memory_space=pltpu.VMEM)
    dma = pltpu.SemaphoreType.DMA
    field_final, membranes = pl.pallas_call(
        fused_kernel,
        out_shape=(jax.ShapeDtypeStruct((trials, regions, 32), F32), jax.ShapeDtypeStruct((rows, slots), F32)),
        in_specs=[pl.BlockSpec(memory_space=pltpu.SMEM)] + [vmem] * 7,
        out_specs=(vmem, vmem),
        scratch_shapes=[
            pltpu.VMEM((regions, slots), F32),
            pltpu.VMEM((1024, LANES), jnp.int32),
            pltpu.VMEM((1024, LANES), F32),
            pltpu.VMEM((8, 1024, slots), BF16),
            pltpu.VMEM((160, slots), BF16),
            pltpu.VMEM((8, 160, slots), F32),
            pltpu.VMEM((8, 2, 8, ROWS, LANES), BF16),
            pltpu.VMEM((8, 2, 8, ROWS, LANES), BF16),
            pltpu.VMEM((12, 8, LANES), F32),
            pltpu.VMEM((16, 8, LANES), F32),
            pltpu.VMEM((8, 8, ROWS, LANES), BF16),
            pltpu.VMEM((2, 4, 4, 2, ROWS, LANES), BF16),
            pltpu.VMEM((2, 4, 4, 2, ROWS, LANES), BF16),
            pltpu.VMEM((4, 12, 8, LANES), F32),
            pltpu.VMEM((4, 8, 8, LANES), F32),
            pltpu.VMEM((12, 8, LANES), F32),
            pltpu.VMEM((8, 8, LANES), F32),
            pltpu.VMEM((12, 8, LANES), F32),
            pltpu.VMEM((8, 8, LANES), F32),
            pltpu.VMEM((12, 8, LANES), F32),
            pltpu.VMEM((8, 8, LANES), F32),
            pltpu.VMEM((8, 12, 8, LANES), F32),
            pltpu.VMEM((8, 8, LANES), F32),
            pltpu.VMEM((640, LANES), F32),
            pltpu.VMEM((8, ROWS, LANES), BF16),
            pltpu.VMEM((2, 8, 32, LANES), BF16),
            pltpu.VMEM((16, ROWS, LANES), BF16),
            pltpu.VMEM((16, 32, LANES), BF16),
            pltpu.VMEM((STEPS, 64, LANES), F32),
            pltpu.VMEM((25, 64, LANES), F32),
            pltpu.VMEM((STEPS, 64, LANES), F32),
            pltpu.VMEM((8, 48, LANES), BF16),
            pltpu.VMEM((16, 48, LANES), BF16),
            pltpu.VMEM((640, LANES), F32),
            pltpu.VMEM((64, LANES), F32),
            pltpu.VMEM((16, 8, LANES), F32),
            dma((4,)), dma((4,)), dma((2, 4, 4)), dma((2, 4, 4)), dma((8,)), dma((8,)),
            dma((2,)), dma((2,)), dma((2, 8)), dma((2, 8)), dma((2, 16)), dma((2, 16)), dma((16,)), dma((16,)),
            dma((16,)), dma((16,)), dma((2, 4, 3)), dma((2, 4, 3)), dma((2, 4)), dma((2, 4)), dma((33,)), dma((33,)),
        ],
        compiler_params=pltpu.CompilerParams(vmem_limit_bytes=VMEM_LIMIT, collective_id=0, has_side_effects=True),
        name="window",
    )(
        region_live, spike_bins.reshape(rows, slots), neuron_site, efficacy,
        membrane_init.reshape(rows, slots), field_init, rim_weights, rim_codes,
    )
    return field_final, membranes.reshape(trials, regions, slots)


def solution(mesh):
    in_specs = (
        P(None, "neur", "surf"),
        P("neur", "surf"),
        P("neur", "surf"),
        P("neur"),
        P(None, "neur", "surf"),
        P(None, "neur", "surf"),
        P(None, "neur", "surf"),
        P(None, "neur", "surf"),
    )
    out_specs = (P(None, "neur", "surf"), P(None, "neur", "surf"))
    return jax.shard_map(local, mesh=mesh, in_specs=in_specs, out_specs=out_specs, check_vma=False)
```

```python
import math

import jax
import jax.numpy as jnp
from jax import lax
from jax.experimental import pallas as pl
from jax.experimental.pallas import tpu as pltpu
from jax.sharding import PartitionSpec as P

STEPS = 10
RIM = 2
FOOT = 8
TAPS = (0.84375, 0.51171875, 0.310546875, 0.1884765625, 0.1142578125, 0.0693359375, 0.0419921875, 0.025390625)
SCALE = 1.0 / sum(TAPS)
DECAY = math.exp(-0.35)
F32 = jnp.float32
BF16 = jnp.bfloat16
VMEM_LIMIT = 56 * 1024 * 1024
ROWS = 80
LANES = 128


def build_band(site, band_ref):
    total, slots = band_ref.shape[-2:]
    tiles = total // 16
    high = jnp.broadcast_to((site >> 4).astype(F32).astype(BF16), (16, slots))
    low = jnp.broadcast_to(site & 15, (16, slots))
    row = lax.broadcasted_iota(jnp.int32, (16, slots), 0)
    first = jnp.zeros((16, slots), F32)
    second = jnp.zeros((16, slots), F32)
    for offset in range(FOOT):
        first = jnp.where(row - low == offset, TAPS[offset], first)
        second = jnp.where(row + 16 - low == offset, TAPS[offset], second)
    first, second = first.astype(BF16), second.astype(BF16)
    zero = jnp.zeros((16, slots), BF16)
    for tile in range(tiles):
        here = high == jnp.asarray(tile, BF16)
        before = high == jnp.asarray((tile - 1) % tiles, BF16)
        band_ref[tile * 16 : tile * 16 + 16, :] = jnp.where(here, first, jnp.where(before, second, zero))


def fused_kernel(
    live_ref, bins_ref, site_ref, eff_ref, start_ref, field_ref, weights_ref, codes_ref,
    ff_ref, out_ref,
    weff_ref, tbins_ref, tstart_ref, band_ref, charge_ref, drive_ref, s_ref, g_ref, rim_ref, init_ref,
    cx_ref, sbuf, rbuf, rq_ref, iq_ref, tl_ref, til_ref, th_ref, tih_ref, tm_ref, tim_ref, ro_ref, io_ref, p_ref, mb_ref, mh_ref,
    own_ref, hal_ref, inj_ref, cf_ref, hist_ref, mb2_ref, h2_ref, t_ref, ffs_ref, ffr_ref,
    cx_send, cx_recv, ring_send, ring_recv, q_send, q_recv, n_send, n_recv, r2_send, r2_recv, a_send, a_recv,
    b_send, b_recv, f_send, f_recv, ag_send, ag_recv, ac_send, ac_recv,
):
    s = lax.axis_index("surf")
    g = lax.axis_index("neur")
    z = s // 4
    yh = (s // 2) % 2
    c = s % 2
    dzh = 2 * yh - 1

    def dev(zz, yy, cc, gg):
        return {"surf": lax.rem(zz + 16, 8) * 4 + yy * 2 + cc, "neur": gg}

    def rdma(src, dst, ss, rs, target):
        return pltpu.make_async_remote_copy(
            src_ref=src, dst_ref=dst, send_sem=ss, recv_sem=rs, device_id=target, device_id_type=pl.DeviceIdType.MESH
        )

    def zmod(dz):
        return lax.rem(z + dz + 16, 8)

    def gmod(i):
        return lax.rem(g + i, 8)

    barrier = pltpu.get_barrier_semaphore()
    me = (yh * 2 + c) * 8 + g

    def greet_plane(i, carry):
        other = lax.rem(me + i, 32)
        pl.semaphore_signal(
            barrier, inc=1, device_id=dev(z, other // 16, (other // 8) % 2, other % 8), device_id_type=pl.DeviceIdType.MESH
        )
        return carry

    lax.fori_loop(1, 32, greet_plane, 0)

    def greet_near(i, carry):
        pl.semaphore_signal(
            barrier, inc=1, device_id=dev(z + dzh, i // 8, c, i % 8), device_id_type=pl.DeviceIdType.MESH
        )
        return carry

    lax.fori_loop(0, 16, greet_near, 0)
    pl.semaphore_signal(barrier, inc=1, device_id=dev(z - dzh, yh, c, g), device_id_type=pl.DeviceIdType.MESH)

    slots = site_ref.shape[1]
    slot_id = s * slots + lax.broadcasted_iota(jnp.int32, (1, slots), 1)

    for tile in range(8):
        tbins_ref[tile * 128 : tile * 128 + 128, :] = bins_ref[:, tile * LANES : tile * LANES + LANES]
        tstart_ref[tile * 128 : tile * 128 + 128, :] = start_ref[:, tile * LANES : tile * LANES + LANES]

    weff_ref[...] = eff_ref[...].astype(F32)

    def trials_of(ref, half, region):
        first = half * 64 + region
        return jnp.concatenate([ref[pl.ds(tile * 128 + first, 8, stride=8), :] for tile in range(8)], axis=1)

    def spread(region, lot):
        weight = jnp.where(slot_id < live_ref[region], weff_ref[pl.ds(region, 1), :], 0.0)
        weight = jnp.broadcast_to(weight, (8, slots))
        band = band_ref.at[region]
        build_band(site_ref[pl.ds(region, 1), :], band)
        for half in range(2):
            bins = trials_of(tbins_ref, half, region)
            for pair in range(STEPS // 2):
                rows = [jnp.where(bins == 2 * pair + j, weight, 0.0) for j in range(2)]
                start = half * ROWS + pair * 16
                charge_ref[lot, start : start + 16, :] = jnp.concatenate(rows, axis=0).astype(BF16)
        total = lax.dot_general(charge_ref[lot], band[...], (((1,), (1,)), ((), ())), preferred_element_type=F32)
        total = (total * SCALE).astype(BF16)
        for plane in range(8):
            for half in range(2):
                s_ref[plane, half, region] = total[half * ROWS : half * ROWS + ROWS, plane * LANES : plane * LANES + LANES]

    partner = dev(z, yh, 1 - c, g)
    cx = {}

    def quarter(index):
        for lot in range(2):
            spread(2 * index + lot, lot)

    def to_partner(index):
        part = pl.ds(2 * index, 2)
        cx[index] = rdma(s_ref.at[:, 1 - c, part], cx_ref.at[:, part], cx_send.at[index], cx_recv.at[index], partner)
        cx[index].start()

    quarter(0)
    pl.semaphore_wait(barrier, 31 + 17)
    to_partner(0)

    q = yh * 2 + c
    for k in range(6):
        rim_ref[k] = jnp.concatenate([weights_ref[k]] * 4, axis=1)
        rim_ref[6 + k] = jnp.concatenate([codes_ref[k].astype(F32)] * 4, axis=1)
    for k in range(16):
        init_ref[k] = jnp.concatenate([field_ref[k]] * 4, axis=1)
    quad = []
    for i in range(1, 4):
        y2 = lax.rem(yh + i // 2, 2)
        c2 = lax.rem(c + i % 2, 2)
        target = dev(z, y2, c2, g)
        quad.append((y2 * 2 + c2, rdma(rim_ref, rq_ref.at[q], q_send.at[i], q_recv.at[q], target)))
        quad.append((y2 * 2 + c2, rdma(init_ref.at[pl.ds(c2 * 8, 8)], iq_ref.at[q], q_send.at[4 + i], q_recv.at[4 + q], target)))
    for _, copy in quad:
        copy.start()
    rq_ref[q] = rim_ref[...]
    iq_ref[q] = init_ref[pl.ds(c * 8, 8)]


    def x_of(dz, index):
        zd = zmod(dz)
        part = slice(2 * index, 2 * index + 2)
        return s_ref[zd, c, part].astype(F32) + cx_ref[zd, part].astype(F32)

    ring = {}

    def hop(index, k):
        for way, sign in ((0, 1), (1, -1)):
            first = 4 if way == index % 2 else 3
            if k >= first:
                continue
            value = x_of(sign * (first - k), index)
            if k == 0:
                pass
            else:
                ring[(way, index, k - 1)].wait_recv()
                value = value + rbuf[way, index, k - 1].astype(F32)
            sbuf[way, index, k] = value.astype(BF16)
            copy = rdma(
                sbuf.at[way, index, k], rbuf.at[way, index, k], ring_send.at[way, index, k], ring_recv.at[way, index, k],
                dev(z + sign, yh, c, g),
            )
            copy.start()
            ring[(way, index, k)] = copy

    quarter(1)
    to_partner(1)
    cx[0].wait_recv()
    hop(0, 0)
    quarter(2)
    to_partner(2)
    cx[1].wait_recv()
    hop(1, 0)
    hop(0, 1)
    quarter(3)
    to_partner(3)
    cx[2].wait_recv()
    hop(2, 0)
    hop(1, 1)
    hop(0, 2)

    lane = lax.broadcasted_iota(jnp.int32, (8, LANES), 1)
    for i in range(1, 4):
        y2 = lax.rem(yh + i // 2, 2)
        c2 = lax.rem(c + i % 2, 2)
        src = y2 * 2 + c2
        rdma(rim_ref, rq_ref.at[src], q_send.at[i], q_recv.at[src], partner).wait_recv()
        rdma(init_ref.at[pl.ds(0, 8)], iq_ref.at[src], q_send.at[4 + i], q_recv.at[4 + src], partner).wait_recv()
    block = lane // 32
    for k in range(12):
        tl_ref[k] = jnp.where(
            block < 2,
            jnp.where(block == 0, rq_ref[0, k], rq_ref[1, k]),
            jnp.where(block == 2, rq_ref[2, k], rq_ref[3, k]),
        )
    for k in range(8):
        til_ref[k] = jnp.where(
            block < 2,
            jnp.where(block == 0, iq_ref[0, k], iq_ref[1, k]),
            jnp.where(block == 2, iq_ref[2, k], iq_ref[3, k]),
        )

    near = (
        rdma(tl_ref, th_ref, n_send.at[0], n_recv.at[0], dev(z - dzh, yh, c, g)),
        rdma(til_ref, tih_ref, n_send.at[1], n_recv.at[1], dev(z - dzh, yh, c, g)),
    )
    for copy in near:
        copy.start()

    def setup_own(i):
        gg = gmod(i)
        target = dev(z, yh, c, gg)
        return (
            rdma(tm_ref, ro_ref.at[g], r2_send.at[0, i], r2_recv.at[0, g], target),
            rdma(tim_ref.at[gg], io_ref.at[g], r2_send.at[1, i], r2_recv.at[1, g], target),
        )

    def start_all(make):
        def body(i, carry):
            for copy in make(i):
                copy.start()
            return carry

        return body

    def sent_all(make):
        def body(i, carry):
            for copy in make(i):
                copy.wait_send()
            return carry

        return body

    cx[3].wait_recv()
    hop(3, 0)
    hop(2, 1)
    hop(1, 2)

    mine = (lane >= 32 * yh) & (lane < 96 + 32 * yh)
    for copy in near:
        copy.wait_recv()
    for k in range(12):
        tm_ref[k] = jnp.where(mine, tl_ref[k], th_ref[k])
    for k in range(8):
        tim_ref[k] = jnp.where(mine, til_ref[k], tih_ref[k])
    lax.fori_loop(1, 8, start_all(setup_own), 0)
    ro_ref[g] = tm_ref[...]
    io_ref[g] = tim_ref[g]

    hop(0, 3)
    hop(3, 1)
    hop(2, 2)

    hop(1, 3)
    hop(3, 2)
    hop(2, 3)
    hop(3, 3)

    def setup_arrived(i, carry):
        gg = gmod(i)
        rdma(tm_ref, ro_ref.at[gg], r2_send.at[0, i], r2_recv.at[0, gg], partner).wait_recv()
        rdma(tim_ref.at[0], io_ref.at[gg], r2_send.at[1, i], r2_recv.at[1, gg], partner).wait_recv()
        return carry

    lax.fori_loop(1, 8, setup_arrived, 0)
    row8 = lax.broadcasted_iota(jnp.int32, (8, LANES), 0)

    def couple(gg, carry):
        weights = [ro_ref[gg, k] for k in range(6)]
        codes = [ro_ref[gg, 6 + k] for k in range(6)]
        rows = pl.ds(pl.multiple_of(gg * 8, 8), 8)
        region = gg * 8 + row8
        for a in range(-RIM, RIM + 1):
            inside = (region + a >= 0) & (region + a < 64)
            for b in range(-RIM, RIM + 1):
                code = (a + RIM) * (2 * RIM + 1) + b + RIM
                if a == 0 and b == 0:
                    cf_ref[code, rows] = 0.9 - 0.15 * (weights[0] + weights[1] + weights[2] + weights[3] + weights[4] + weights[5])
                    continue
                total = jnp.zeros((8, LANES), F32)
                for k in range(6):
                    total = total + jnp.where(codes[k] == float(code), weights[k], 0.0)
                cf_ref[code, rows] = jnp.where(inside, 0.15 * total, 0.0)
        ffs_ref[rows] = io_ref[gg]
        return carry

    lax.fori_loop(0, 8, couple, 0)
    for a in range(-RIM, RIM + 1):
        if a != 0:
            for b in range(2 * RIM + 1):
                code = (a + RIM) * (2 * RIM + 1) + b
                cf_ref[code] = pltpu.roll(cf_ref[code], a % 64, 0)

    for index in range(4):
        value = x_of(0, index)
        for way in range(2):
            k = 3 if way == index % 2 else 2
            ring[(way, index, k)].wait_recv()
            value = value + rbuf[way, index, k].astype(F32)
        p_ref[index * 160 : index * 160 + 160, :] = value.reshape(160, LANES)

    lane16 = lax.broadcasted_iota(jnp.int32, (16, LANES), 1)
    block16 = lane16 // 32

    def by_block(tiles):
        return jnp.where(
            block16 < 2, jnp.where(block16 == 0, tiles[0], tiles[1]), jnp.where(block16 == 2, tiles[2], tiles[3])
        )

    slot = yh * 8 + g

    def trial_own(k):
        n = gmod(k % 8)
        return (rdma(mb_ref.at[n], own_ref.at[slot], a_send.at[0, k], a_recv.at[0, slot], dev(z, lax.rem(yh + k // 8, 2), c, n)),)

    def trial_near(k):
        n = gmod(k % 8)
        up = k // 8
        return (rdma(mh_ref.at[up, n], hal_ref.at[slot], a_send.at[1, k], a_recv.at[1, slot], dev(z + 1 - 2 * up, up, c, n)),)

    def trial_send(i, carry):
        n = gmod(i)
        tiles = []
        for pair in range(STEPS // 2):
            parts = [p_ref[pl.ds((2 * pair + j) * 8 + n, 8, stride=ROWS), :] for j in range(2)]
            tiles.append(jnp.concatenate(parts, axis=0))
            mb_ref[n, pair * 16 : pair * 16 + 16] = tiles[-1].astype(BF16)
        high = [pltpu.roll(tiles[j], 32 * j + 32, 1) if j < 3 else tiles[j] for j in range(4)]
        low = [pltpu.roll(tiles[j], 32 * j, 1) if j > 0 else tiles[j] for j in range(4)]
        mh_ref[0, n, :16] = by_block(high).astype(BF16)
        mh_ref[1, n, :16] = by_block(low).astype(BF16)
        mh_ref[0, n, 16:] = tiles[4].astype(BF16)
        mh_ref[1, n, 16:] = tiles[4].astype(BF16)
        trial_own(i + 8)[0].start()
        trial_near(i)[0].start()
        trial_near(i + 8)[0].start()

        @pl.when(i > 0)
        def _():
            trial_own(i)[0].start()

        return carry

    lax.fori_loop(1, 8, trial_send, 0)
    trial_send(0, 0)
    own_ref[slot] = mb_ref[g]

    def trial_arrived(k, carry):
        @pl.when(k != slot)
        def _():
            rdma(mb_ref.at[0], own_ref.at[k], a_send.at[0, 0], a_recv.at[0, k], partner).wait_recv()

        rdma(mh_ref.at[0, 0], hal_ref.at[k], a_send.at[1, 0], a_recv.at[1, k], partner).wait_recv()
        return carry

    lax.fori_loop(0, 16, trial_arrived, 0)
    mine16 = (lane16 >= 32 * yh) & (lane16 < 96 + 32 * yh)

    def unpack(gg, carry):
        rows = pl.ds(pl.multiple_of(gg * 8, 8), 8)
        edge = hal_ref[gg].astype(F32) + hal_ref[8 + gg].astype(F32)
        for pair in range(STEPS // 2):
            tile = slice(pair * 16, pair * 16 + 16)
            near_edge = pltpu.roll(edge[:16], lax.rem(96 * (1 - yh) - 32 * pair + 128, 128), 1) if pair < 4 else edge[16:]
            value = jnp.where(mine16, own_ref[gg, tile].astype(F32) + own_ref[8 + gg, tile].astype(F32), near_edge)
            inj_ref[2 * pair, rows] = value[:8]
            inj_ref[2 * pair + 1, rows] = value[8:]
        return carry

    lax.fori_loop(0, 8, unpack, 0)

    def advance(step, carry):
        field, rate = carry
        rate = DECAY * rate + inj_ref[step]
        total = 0.1 * rate
        shifted = [field if b == 0 else pltpu.roll(field, (-b) % LANES, 1) for b in range(-RIM, RIM + 1)]
        for a in range(-RIM, RIM + 1):
            term = None
            for b in range(2 * RIM + 1):
                product = cf_ref[(a + RIM) * (2 * RIM + 1) + b] * shifted[b]
                term = product if term is None else term + product
            total = total + (term if a == 0 else pltpu.roll(term, (-a) % 64, 0))
        hist_ref[step] = total
        return (total, rate)

    last, _ = lax.fori_loop(0, STEPS, advance, (ffs_ref[...], jnp.zeros((64, LANES), F32)))
    ffs_ref[...] = last

    mine64 = (lane16 >= 64 * yh) & (lane16 < 64 + 64 * yh)

    trial = c * 8 + g

    def back(k):
        gg = gmod(k % 8)
        return (rdma(mb2_ref.at[gg], h2_ref.at[slot], b_send.at[k], b_recv.at[slot], dev(z, lax.rem(yh + k // 8, 2), c, gg)),)

    def final(k):
        gg = gmod(k % 8)
        rows = pl.ds(pl.multiple_of(gg * 8, 8), 8)
        return (rdma(ffs_ref.at[rows], ffr_ref.at[trial], f_send.at[k], f_recv.at[trial], dev(z, yh, lax.rem(c + k // 8, 2), gg)),)

    def pack(i, carry):
        gg = gmod(i)
        rows = pl.ds(pl.multiple_of(gg * 8, 8), 8)
        tiles = [
            jnp.concatenate([hist_ref[2 * pair, rows], hist_ref[2 * pair + 1, rows]], axis=0) for pair in range(STEPS // 2)
        ]
        for m in range(2):
            both = jnp.where(mine64, tiles[2 * m], pltpu.roll(tiles[2 * m + 1], 64, 1))
            mb2_ref[gg, m * 16 : m * 16 + 16] = both.astype(BF16)
        mb2_ref[gg, 32:48] = tiles[4].astype(BF16)
        back(i + 8)[0].start()

        @pl.when(i > 0)
        def _():
            back(i)[0].start()

        return carry

    lax.fori_loop(1, 8, pack, 0)
    pack(0, 0)
    lax.fori_loop(1, 16, start_all(final), 0)
    h2_ref[slot] = mb2_ref[g]
    ffr_ref[trial] = ffs_ref[pl.ds(pl.multiple_of(g * 8, 8), 8)]

    def back_arrived(k, carry):
        @pl.when(k != slot)
        def _():
            rdma(mb2_ref.at[0], h2_ref.at[k], b_send.at[0], b_recv.at[k], partner).wait_recv()

        return carry

    lax.fori_loop(0, 16, back_arrived, 0)
    for n in range(8):
        for m in range(3):
            tile = slice(m * 16, m * 16 + 16)
            left, right = h2_ref[n, tile].astype(F32), h2_ref[8 + n, tile].astype(F32)
            t_ref[pl.ds(2 * m * 128 + n, 16, stride=8), :] = jnp.where(lane16 < 64, left, right)
            if m < 2:
                t_ref[pl.ds((2 * m + 1) * 128 + n, 16, stride=8), :] = pltpu.roll(jnp.where(lane16 < 64, right, left), 64, 1)
    for r in range(8):
        for pair in range(STEPS // 2):
            parts = [t_ref[(2 * pair + j) * 64 + r * 8 : (2 * pair + j) * 64 + r * 8 + 8, :] for j in range(2)]
            g_ref[z, c, r, pair * 16 : pair * 16 + 16] = jnp.concatenate(parts, axis=0).astype(BF16)

    quarters = (0, 1, 2, 3)
    ag, ac = {}, []

    def piece(zz, half, index):
        return g_ref.at[zz, half, pl.ds(2 * index, 2)]

    def source(way, k):
        return zmod(-1 - k if way == 0 else 1 + k)

    def arrives(way, k, i):
        return k < 3 or (way == 0 and i < 2) or (way == 1 and i >= 2)

    def pass_on(way, k, i):
        zz = z if k == 0 else source(way, k - 1)
        part = piece(zz, c, quarters[i])
        copy = rdma(part, part, ag_send.at[way, k, i], ag_recv.at[way, k, i], dev(z + 1 - 2 * way, yh, c, g))
        copy.start()
        ag[(way, k, i)] = copy

    def to_core(part, other, index, k):
        copy = rdma(part, part, ac_send.at[index], ac_recv.at[index], partner)
        copy.start()
        ac.append((copy, rdma(other, other, ac_send.at[index], ac_recv.at[index], partner), k))

    def share(way, k, i):
        zz = source(way, k)
        part = piece(zz, c, quarters[i])
        to_core(part, piece(zz, 1 - c, quarters[i]), (way * 4 + k) * 4 + i, k)

    for i in range(4):
        for way in range(2):
            pass_on(way, 0, i)
    own_part, own_other = g_ref.at[z, c], g_ref.at[z, 1 - c]
    own_copy = rdma(own_part, own_part, ac_send.at[32], ac_recv.at[32], partner)
    own_copy.start()

    def final_arrived(k, carry):
        @pl.when(k != trial)
        def _():
            rdma(ffs_ref.at[pl.ds(0, 8)], ffr_ref.at[k], f_send.at[0], f_recv.at[k], partner).wait_recv()

        return carry

    lax.fori_loop(0, 16, final_arrived, 0)
    for k in range(16):
        value = pltpu.roll(ffr_ref[k], lax.rem(128 - 32 * q, 128), 1)
        ff_ref[k] = value[:, :32]

    for k in range(1, 4):
        for i in range(4):
            for way in range(2):
                if arrives(way, k, i):
                    ag[(way, k - 1, i)].wait_recv()
                    pass_on(way, k, i)
                    share(way, k - 1, i)
        for i in range(4):
            for way in range(2):
                if not arrives(way, k, i):
                    ag[(way, k - 1, i)].wait_recv()
                    share(way, k - 1, i)

    near_planes = (z, zmod(1), zmod(-1), zmod(2), zmod(-2))
    far_planes = (zmod(3), zmod(-3), zmod(4))

    def product(region, planes):
        history = jnp.concatenate(
            [jnp.concatenate([g_ref[plane, 0, region], g_ref[plane, 1, region]], axis=0) for plane in planes], axis=1
        )
        band = jnp.concatenate(
            [band_ref[region, pl.ds(pl.multiple_of(plane * LANES, LANES), LANES), :] for plane in planes], axis=0
        )
        return jnp.dot(history, band, preferred_element_type=F32)

    def collect_near(region, carry):
        drive_ref[region] = product(region, near_planes)
        return carry

    rdma(own_other, own_other, ac_send.at[32], ac_recv.at[32], partner).wait_recv()
    for _, other, k in ac:
        if k < 2:
            other.wait_recv()
    lax.fori_loop(0, 4, collect_near, 0)
    for i in range(4):
        for way in range(2):
            if arrives(way, 3, i):
                ag[(way, 3, i)].wait_recv()
                share(way, 3, i)
    lax.fori_loop(4, 8, collect_near, 0)
    for _, other, k in ac:
        if k >= 2:
            other.wait_recv()

    slot8 = s * slots + lax.broadcasted_iota(jnp.int32, (8, slots), 1)

    def collect(region, carry):
        drive_ref[region] = drive_ref[region] + product(region, far_planes)
        live = slot8 < live_ref[region]
        for half in range(2):
            bins = trials_of(tbins_ref, half, region)
            voltage = trials_of(tstart_ref, half, region)
            for step in range(STEPS):
                start = half * ROWS + step * 8
                voltage = 0.9 * voltage + (0.5 * SCALE) * drive_ref[region, start : start + 8, :]
                voltage = jnp.where(bins == step, -0.5, voltage)
            voltage = jnp.where(live, voltage, 0.0)
            for tile in range(8):
                tstart_ref[pl.ds(tile * 128 + half * 64 + region, 8, stride=8), :] = voltage[:, tile * LANES : tile * LANES + LANES]
        return carry

    lax.fori_loop(0, 8, collect, 0)
    for tile in range(8):
        out_ref[:, tile * LANES : tile * LANES + LANES] = tstart_ref[tile * 128 : tile * 128 + 128, :]

    for copy in cx.values():
        copy.wait_send()
    for _, copy in quad:
        copy.wait_send()
    for copy in ring.values():
        copy.wait_send()
    lax.fori_loop(1, 8, sent_all(setup_own), 0)
    for copy in near:
        copy.wait_send()
    lax.fori_loop(1, 16, sent_all(trial_own), 0)
    lax.fori_loop(0, 16, sent_all(trial_near), 0)
    lax.fori_loop(1, 16, sent_all(back), 0)
    lax.fori_loop(1, 16, sent_all(final), 0)
    own_copy.wait_send()
    for copy in ag.values():
        copy.wait_send()
    for copy, _, _ in ac:
        copy.wait_send()


def local(spike_bins, neuron_site, efficacy, region_live, membrane_init, field_init, rim_weights, rim_codes):
    trials, regions, slots = spike_bins.shape
    rows = trials * regions
    vmem = pl.BlockSpec(memory_space=pltpu.VMEM)
    dma = pltpu.SemaphoreType.DMA
    field_final, membranes = pl.pallas_call(
        fused_kernel,
        out_shape=(jax.ShapeDtypeStruct((trials, regions, 32), F32), jax.ShapeDtypeStruct((rows, slots), F32)),
        in_specs=[pl.BlockSpec(memory_space=pltpu.SMEM)] + [vmem] * 7,
        out_specs=(vmem, vmem),
        scratch_shapes=[
            pltpu.VMEM((regions, slots), F32),
            pltpu.VMEM((1024, LANES), jnp.int32),
            pltpu.VMEM((1024, LANES), F32),
            pltpu.VMEM((8, 1024, slots), BF16),
            pltpu.VMEM((2, 160, slots), BF16),
            pltpu.VMEM((8, 160, slots), F32),
            pltpu.VMEM((8, 2, 8, ROWS, LANES), BF16),
            pltpu.VMEM((8, 2, 8, ROWS, LANES), BF16),
            pltpu.VMEM((12, 8, LANES), F32),
            pltpu.VMEM((16, 8, LANES), F32),
            pltpu.VMEM((8, 8, ROWS, LANES), BF16),
            pltpu.VMEM((2, 4, 4, 2, ROWS, LANES), BF16),
            pltpu.VMEM((2, 4, 4, 2, ROWS, LANES), BF16),
            pltpu.VMEM((4, 12, 8, LANES), F32),
            pltpu.VMEM((4, 8, 8, LANES), F32),
            pltpu.VMEM((12, 8, LANES), F32),
            pltpu.VMEM((8, 8, LANES), F32),
            pltpu.VMEM((12, 8, LANES), F32),
            pltpu.VMEM((8, 8, LANES), F32),
            pltpu.VMEM((12, 8, LANES), F32),
            pltpu.VMEM((8, 8, LANES), F32),
            pltpu.VMEM((8, 12, 8, LANES), F32),
            pltpu.VMEM((8, 8, LANES), F32),
            pltpu.VMEM((640, LANES), F32),
            pltpu.VMEM((8, ROWS, LANES), BF16),
            pltpu.VMEM((2, 8, 32, LANES), BF16),
            pltpu.VMEM((16, ROWS, LANES), BF16),
            pltpu.VMEM((16, 32, LANES), BF16),
            pltpu.VMEM((STEPS, 64, LANES), F32),
            pltpu.VMEM((25, 64, LANES), F32),
            pltpu.VMEM((STEPS, 64, LANES), F32),
            pltpu.VMEM((8, 48, LANES), BF16),
            pltpu.VMEM((16, 48, LANES), BF16),
            pltpu.VMEM((640, LANES), F32),
            pltpu.VMEM((64, LANES), F32),
            pltpu.VMEM((16, 8, LANES), F32),
            dma((4,)), dma((4,)), dma((2, 4, 4)), dma((2, 4, 4)), dma((8,)), dma((8,)),
            dma((2,)), dma((2,)), dma((2, 8)), dma((2, 8)), dma((2, 16)), dma((2, 16)), dma((16,)), dma((16,)),
            dma((16,)), dma((16,)), dma((2, 4, 4)), dma((2, 4, 4)), dma((33,)), dma((33,)),
        ],
        compiler_params=pltpu.CompilerParams(vmem_limit_bytes=VMEM_LIMIT, collective_id=0, has_side_effects=True),
        name="window",
    )(
        region_live, spike_bins.reshape(rows, slots), neuron_site, efficacy,
        membrane_init.reshape(rows, slots), field_init, rim_weights, rim_codes,
    )
    return field_final, membranes.reshape(trials, regions, slots)


def solution(mesh):
    in_specs = (
        P(None, "neur", "surf"),
        P("neur", "surf"),
        P("neur", "surf"),
        P("neur"),
        P(None, "neur", "surf"),
        P(None, "neur", "surf"),
        P(None, "neur", "surf"),
        P(None, "neur", "surf"),
    )
    out_specs = (P(None, "neur", "surf"), P(None, "neur", "surf"))
    return jax.shard_map(local, mesh=mesh, in_specs=in_specs, out_specs=out_specs, check_vma=False)
```

```python
import math

import jax
import jax.numpy as jnp
from jax import lax
from jax.experimental import pallas as pl
from jax.experimental.pallas import tpu as pltpu
from jax.sharding import PartitionSpec as P

STEPS = 10
RIM = 2
FOOT = 8
TAPS = (0.84375, 0.51171875, 0.310546875, 0.1884765625, 0.1142578125, 0.0693359375, 0.0419921875, 0.025390625)
SCALE = 1.0 / sum(TAPS)
DECAY = math.exp(-0.35)
F32 = jnp.float32
BF16 = jnp.bfloat16
VMEM_LIMIT = 56 * 1024 * 1024
ROWS = 80
LANES = 128


def build_band(site, band_ref):
    total, slots = band_ref.shape[-2:]
    tiles = total // 16
    high = jnp.broadcast_to((site >> 4).astype(F32).astype(BF16), (16, slots))
    low = jnp.broadcast_to(site & 15, (16, slots))
    row = lax.broadcasted_iota(jnp.int32, (16, slots), 0)
    first = jnp.zeros((16, slots), F32)
    second = jnp.zeros((16, slots), F32)
    for offset in range(FOOT):
        first = jnp.where(row - low == offset, TAPS[offset], first)
        second = jnp.where(row + 16 - low == offset, TAPS[offset], second)
    first, second = first.astype(BF16), second.astype(BF16)
    zero = jnp.zeros((16, slots), BF16)
    for tile in range(tiles):
        here = high == jnp.asarray(tile, BF16)
        before = high == jnp.asarray((tile - 1) % tiles, BF16)
        band_ref[tile * 16 : tile * 16 + 16, :] = jnp.where(here, first, jnp.where(before, second, zero))


def fused_kernel(
    live_ref, bins_ref, site_ref, eff_ref, start_ref, field_ref, weights_ref, codes_ref,
    ff_ref, out_ref,
    weff_ref, tbins_ref, tstart_ref, band_ref, charge_ref, drive_ref, s_ref, g_ref, rim_ref, init_ref,
    cx_ref, sbuf, rbuf, rq_ref, iq_ref, tl_ref, til_ref, th_ref, tih_ref, tm_ref, tim_ref, ro_ref, io_ref, p_ref, mb_ref, mh_ref,
    own_ref, hal_ref, inj_ref, cf_ref, hist_ref, mb2_ref, h2_ref, t_ref, ffs_ref, ffr_ref,
    cx_send, cx_recv, ring_send, ring_recv, q_send, q_recv, n_send, n_recv, r2_send, r2_recv, a_send, a_recv,
    b_send, b_recv, f_send, f_recv, ag_send, ag_recv, ac_send, ac_recv,
):
    s = lax.axis_index("surf")
    g = lax.axis_index("neur")
    z = s // 4
    yh = (s // 2) % 2
    c = s % 2
    dzh = 2 * yh - 1

    def dev(zz, yy, cc, gg):
        return {"surf": lax.rem(zz + 16, 8) * 4 + yy * 2 + cc, "neur": gg}

    def rdma(src, dst, ss, rs, target):
        return pltpu.make_async_remote_copy(
            src_ref=src, dst_ref=dst, send_sem=ss, recv_sem=rs, device_id=target, device_id_type=pl.DeviceIdType.MESH
        )

    def zmod(dz):
        return lax.rem(z + dz + 16, 8)

    def gmod(i):
        return lax.rem(g + i, 8)

    barrier = pltpu.get_barrier_semaphore()

    def greet(target):
        pl.semaphore_signal(barrier, inc=1, device_id=target, device_id_type=pl.DeviceIdType.MESH)

    greet(dev(z, yh, 1 - c, g))
    greet(dev(z, 1 - yh, 1 - c, g))
    greet(dev(z - dzh, yh, c, g))
    for a in range(2):
        for i in range(8):
            if a or i:
                greet(dev(z, lax.rem(yh + a, 2), c, gmod(i)))
            greet(dev(z + dzh, a, c, i))

    slots = site_ref.shape[1]
    slot_id = s * slots + lax.broadcasted_iota(jnp.int32, (1, slots), 1)

    for tile in range(8):
        tbins_ref[tile * 128 : tile * 128 + 128, :] = bins_ref[:, tile * LANES : tile * LANES + LANES]
        tstart_ref[tile * 128 : tile * 128 + 128, :] = start_ref[:, tile * LANES : tile * LANES + LANES]

    weff_ref[...] = eff_ref[...].astype(F32)

    def trials_of(ref, half, region):
        first = half * 64 + region
        return jnp.concatenate([ref[pl.ds(tile * 128 + first, 8, stride=8), :] for tile in range(8)], axis=1)

    def spread(region, lot):
        weight = jnp.where(slot_id < live_ref[region], weff_ref[pl.ds(region, 1), :], 0.0)
        weight = jnp.broadcast_to(weight, (8, slots))
        band = band_ref.at[region]
        build_band(site_ref[pl.ds(region, 1), :], band)
        for half in range(2):
            bins = trials_of(tbins_ref, half, region)
            for pair in range(STEPS // 2):
                rows = [jnp.where(bins == 2 * pair + j, weight, 0.0) for j in range(2)]
                start = half * ROWS + pair * 16
                charge_ref[lot, start : start + 16, :] = jnp.concatenate(rows, axis=0).astype(BF16)
        total = lax.dot_general(charge_ref[lot], band[...], (((1,), (1,)), ((), ())), preferred_element_type=F32)
        total = (total * SCALE).astype(BF16)
        for plane in range(8):
            for half in range(2):
                s_ref[plane, half, region] = total[half * ROWS : half * ROWS + ROWS, plane * LANES : plane * LANES + LANES]

    partner = dev(z, yh, 1 - c, g)
    cx = {}

    def quarter(index):
        for lot in range(2):
            spread(2 * index + lot, lot)

    def to_partner(index):
        part = pl.ds(2 * index, 2)
        cx[index] = rdma(s_ref.at[:, 1 - c, part], cx_ref.at[:, part], cx_send.at[index], cx_recv.at[index], partner)
        cx[index].start()

    quarter(0)
    pl.semaphore_wait(barrier, 2 + 15 + 17)
    to_partner(0)

    q = yh * 2 + c
    for k in range(6):
        rim_ref[k] = jnp.concatenate([weights_ref[k]] * 4, axis=1)
        rim_ref[6 + k] = jnp.concatenate([codes_ref[k].astype(F32)] * 4, axis=1)
    for k in range(16):
        init_ref[k] = jnp.concatenate([field_ref[k]] * 4, axis=1)
    quad = []
    for i in range(1, 4):
        y2 = lax.rem(yh + i // 2, 2)
        c2 = lax.rem(c + i % 2, 2)
        target = dev(z, y2, c2, g)
        quad.append((y2 * 2 + c2, rdma(rim_ref, rq_ref.at[q], q_send.at[i], q_recv.at[q], target)))
        quad.append((y2 * 2 + c2, rdma(init_ref.at[pl.ds(c2 * 8, 8)], iq_ref.at[q], q_send.at[4 + i], q_recv.at[4 + q], target)))
    for _, copy in quad:
        copy.start()
    rq_ref[q] = rim_ref[...]
    iq_ref[q] = init_ref[pl.ds(c * 8, 8)]


    def x_of(dz, index):
        zd = zmod(dz)
        part = slice(2 * index, 2 * index + 2)
        return s_ref[zd, c, part].astype(F32) + cx_ref[zd, part].astype(F32)

    ring = {}

    def hop(index, k):
        for way, sign in ((0, 1), (1, -1)):
            first = 4 if way == index % 2 else 3
            if k >= first:
                continue
            value = x_of(sign * (first - k), index)
            if k == 0:
                pass
            else:
                ring[(way, index, k - 1)].wait_recv()
                value = value + rbuf[way, index, k - 1].astype(F32)
            sbuf[way, index, k] = value.astype(BF16)
            copy = rdma(
                sbuf.at[way, index, k], rbuf.at[way, index, k], ring_send.at[way, index, k], ring_recv.at[way, index, k],
                dev(z + sign, yh, c, g),
            )
            copy.start()
            ring[(way, index, k)] = copy

    quarter(1)
    to_partner(1)
    cx[0].wait_recv()
    hop(0, 0)
    quarter(2)
    to_partner(2)
    cx[1].wait_recv()
    hop(1, 0)
    hop(0, 1)
    quarter(3)
    to_partner(3)
    cx[2].wait_recv()
    hop(2, 0)
    hop(1, 1)
    hop(0, 2)

    lane = lax.broadcasted_iota(jnp.int32, (8, LANES), 1)
    for i in range(1, 4):
        y2 = lax.rem(yh + i // 2, 2)
        c2 = lax.rem(c + i % 2, 2)
        src = y2 * 2 + c2
        rdma(rim_ref, rq_ref.at[src], q_send.at[i], q_recv.at[src], partner).wait_recv()
        rdma(init_ref.at[pl.ds(0, 8)], iq_ref.at[src], q_send.at[4 + i], q_recv.at[4 + src], partner).wait_recv()
    block = lane // 32
    for k in range(12):
        tl_ref[k] = jnp.where(
            block < 2,
            jnp.where(block == 0, rq_ref[0, k], rq_ref[1, k]),
            jnp.where(block == 2, rq_ref[2, k], rq_ref[3, k]),
        )
    for k in range(8):
        til_ref[k] = jnp.where(
            block < 2,
            jnp.where(block == 0, iq_ref[0, k], iq_ref[1, k]),
            jnp.where(block == 2, iq_ref[2, k], iq_ref[3, k]),
        )

    near = (
        rdma(tl_ref, th_ref, n_send.at[0], n_recv.at[0], dev(z - dzh, yh, c, g)),
        rdma(til_ref, tih_ref, n_send.at[1], n_recv.at[1], dev(z - dzh, yh, c, g)),
    )
    for copy in near:
        copy.start()

    def setup_own(i):
        gg = gmod(i)
        target = dev(z, yh, c, gg)
        return (
            rdma(tm_ref, ro_ref.at[g], r2_send.at[0, i], r2_recv.at[0, g], target),
            rdma(tim_ref.at[gg], io_ref.at[g], r2_send.at[1, i], r2_recv.at[1, g], target),
        )

    def start_all(make):
        def body(i, carry):
            for copy in make(i):
                copy.start()
            return carry

        return body

    def sent_all(make):
        def body(i, carry):
            for copy in make(i):
                copy.wait_send()
            return carry

        return body

    cx[3].wait_recv()
    hop(3, 0)
    hop(2, 1)
    hop(1, 2)

    mine = (lane >= 32 * yh) & (lane < 96 + 32 * yh)
    for copy in near:
        copy.wait_recv()
    for k in range(12):
        tm_ref[k] = jnp.where(mine, tl_ref[k], th_ref[k])
    for k in range(8):
        tim_ref[k] = jnp.where(mine, til_ref[k], tih_ref[k])
    lax.fori_loop(1, 8, start_all(setup_own), 0)
    ro_ref[g] = tm_ref[...]
    io_ref[g] = tim_ref[g]

    hop(0, 3)
    hop(3, 1)
    hop(2, 2)

    hop(1, 3)
    hop(3, 2)
    hop(2, 3)
    hop(3, 3)

    def setup_arrived(i, carry):
        gg = gmod(i)
        rdma(tm_ref, ro_ref.at[gg], r2_send.at[0, i], r2_recv.at[0, gg], partner).wait_recv()
        rdma(tim_ref.at[0], io_ref.at[gg], r2_send.at[1, i], r2_recv.at[1, gg], partner).wait_recv()
        return carry

    lax.fori_loop(1, 8, setup_arrived, 0)
    row8 = lax.broadcasted_iota(jnp.int32, (8, LANES), 0)

    def couple(gg, carry):
        weights = [ro_ref[gg, k] for k in range(6)]
        codes = [ro_ref[gg, 6 + k] for k in range(6)]
        rows = pl.ds(pl.multiple_of(gg * 8, 8), 8)
        region = gg * 8 + row8
        for a in range(-RIM, RIM + 1):
            inside = (region + a >= 0) & (region + a < 64)
            for b in range(-RIM, RIM + 1):
                code = (a + RIM) * (2 * RIM + 1) + b + RIM
                if a == 0 and b == 0:
                    cf_ref[code, rows] = 0.9 - 0.15 * (weights[0] + weights[1] + weights[2] + weights[3] + weights[4] + weights[5])
                    continue
                total = jnp.zeros((8, LANES), F32)
                for k in range(6):
                    total = total + jnp.where(codes[k] == float(code), weights[k], 0.0)
                cf_ref[code, rows] = jnp.where(inside, 0.15 * total, 0.0)
        ffs_ref[rows] = io_ref[gg]
        return carry

    lax.fori_loop(0, 8, couple, 0)
    for a in range(-RIM, RIM + 1):
        if a != 0:
            for b in range(2 * RIM + 1):
                code = (a + RIM) * (2 * RIM + 1) + b
                cf_ref[code] = pltpu.roll(cf_ref[code], a % 64, 0)

    for index in range(4):
        value = x_of(0, index)
        for way in range(2):
            k = 3 if way == index % 2 else 2
            ring[(way, index, k)].wait_recv()
            value = value + rbuf[way, index, k].astype(F32)
        p_ref[index * 160 : index * 160 + 160, :] = value.reshape(160, LANES)

    lane16 = lax.broadcasted_iota(jnp.int32, (16, LANES), 1)
    block16 = lane16 // 32

    def by_block(tiles):
        return jnp.where(
            block16 < 2, jnp.where(block16 == 0, tiles[0], tiles[1]), jnp.where(block16 == 2, tiles[2], tiles[3])
        )

    slot = yh * 8 + g

    def trial_own(k):
        n = gmod(k % 8)
        return (rdma(mb_ref.at[n], own_ref.at[slot], a_send.at[0, k], a_recv.at[0, slot], dev(z, lax.rem(yh + k // 8, 2), c, n)),)

    def trial_near(k):
        n = gmod(k % 8)
        up = k // 8
        return (rdma(mh_ref.at[up, n], hal_ref.at[slot], a_send.at[1, k], a_recv.at[1, slot], dev(z + 1 - 2 * up, up, c, n)),)

    def trial_send(i, carry):
        n = gmod(i)
        tiles = []
        for pair in range(STEPS // 2):
            parts = [p_ref[pl.ds((2 * pair + j) * 8 + n, 8, stride=ROWS), :] for j in range(2)]
            tiles.append(jnp.concatenate(parts, axis=0))
            mb_ref[n, pair * 16 : pair * 16 + 16] = tiles[-1].astype(BF16)
        high = [pltpu.roll(tiles[j], 32 * j + 32, 1) if j < 3 else tiles[j] for j in range(4)]
        low = [pltpu.roll(tiles[j], 32 * j, 1) if j > 0 else tiles[j] for j in range(4)]
        mh_ref[0, n, :16] = by_block(high).astype(BF16)
        mh_ref[1, n, :16] = by_block(low).astype(BF16)
        mh_ref[0, n, 16:] = tiles[4].astype(BF16)
        mh_ref[1, n, 16:] = tiles[4].astype(BF16)
        trial_own(i + 8)[0].start()
        trial_near(i)[0].start()
        trial_near(i + 8)[0].start()

        @pl.when(i > 0)
        def _():
            trial_own(i)[0].start()

        return carry

    lax.fori_loop(1, 8, trial_send, 0)
    trial_send(0, 0)
    own_ref[slot] = mb_ref[g]

    def trial_arrived(k, carry):
        @pl.when(k != slot)
        def _():
            rdma(mb_ref.at[0], own_ref.at[k], a_send.at[0, 0], a_recv.at[0, k], partner).wait_recv()

        rdma(mh_ref.at[0, 0], hal_ref.at[k], a_send.at[1, 0], a_recv.at[1, k], partner).wait_recv()
        return carry

    lax.fori_loop(0, 16, trial_arrived, 0)
    mine16 = (lane16 >= 32 * yh) & (lane16 < 96 + 32 * yh)

    def unpack(gg, carry):
        rows = pl.ds(pl.multiple_of(gg * 8, 8), 8)
        edge = hal_ref[gg].astype(F32) + hal_ref[8 + gg].astype(F32)
        for pair in range(STEPS // 2):
            tile = slice(pair * 16, pair * 16 + 16)
            near_edge = pltpu.roll(edge[:16], lax.rem(96 * (1 - yh) - 32 * pair + 128, 128), 1) if pair < 4 else edge[16:]
            value = jnp.where(mine16, own_ref[gg, tile].astype(F32) + own_ref[8 + gg, tile].astype(F32), near_edge)
            inj_ref[2 * pair, rows] = value[:8]
            inj_ref[2 * pair + 1, rows] = value[8:]
        return carry

    lax.fori_loop(0, 8, unpack, 0)

    def advance(step, carry):
        field, rate = carry
        rate = DECAY * rate + inj_ref[step]
        total = 0.1 * rate
        shifted = [field if b == 0 else pltpu.roll(field, (-b) % LANES, 1) for b in range(-RIM, RIM + 1)]
        for a in range(-RIM, RIM + 1):
            term = None
            for b in range(2 * RIM + 1):
                product = cf_ref[(a + RIM) * (2 * RIM + 1) + b] * shifted[b]
                term = product if term is None else term + product
            total = total + (term if a == 0 else pltpu.roll(term, (-a) % 64, 0))
        hist_ref[step] = total
        return (total, rate)

    last, _ = lax.fori_loop(0, STEPS, advance, (ffs_ref[...], jnp.zeros((64, LANES), F32)))
    ffs_ref[...] = last

    mine64 = (lane16 >= 64 * yh) & (lane16 < 64 + 64 * yh)

    trial = c * 8 + g

    def back(k):
        gg = gmod(k % 8)
        return (rdma(mb2_ref.at[gg], h2_ref.at[slot], b_send.at[k], b_recv.at[slot], dev(z, lax.rem(yh + k // 8, 2), c, gg)),)

    def final(k):
        gg = gmod(k % 8)
        rows = pl.ds(pl.multiple_of(gg * 8, 8), 8)
        return (rdma(ffs_ref.at[rows], ffr_ref.at[trial], f_send.at[k], f_recv.at[trial], dev(z, yh, c, gg)),)

    def pack(i, carry):
        gg = gmod(i)
        rows = pl.ds(pl.multiple_of(gg * 8, 8), 8)
        tiles = [
            jnp.concatenate([hist_ref[2 * pair, rows], hist_ref[2 * pair + 1, rows]], axis=0) for pair in range(STEPS // 2)
        ]
        for m in range(2):
            both = jnp.where(mine64, tiles[2 * m], pltpu.roll(tiles[2 * m + 1], 64, 1))
            mb2_ref[gg, m * 16 : m * 16 + 16] = both.astype(BF16)
        mb2_ref[gg, 32:48] = tiles[4].astype(BF16)
        back(i + 8)[0].start()

        @pl.when(i > 0)
        def _():
            back(i)[0].start()

        return carry

    lax.fori_loop(1, 8, pack, 0)
    pack(0, 0)
    lax.fori_loop(1, 8, start_all(final), 0)
    h2_ref[slot] = mb2_ref[g]
    ffr_ref[trial] = ffs_ref[pl.ds(pl.multiple_of(g * 8, 8), 8)]

    def back_arrived(k, carry):
        @pl.when(k != slot)
        def _():
            rdma(mb2_ref.at[0], h2_ref.at[k], b_send.at[0], b_recv.at[k], partner).wait_recv()

        return carry

    lax.fori_loop(0, 16, back_arrived, 0)
    for n in range(8):
        for m in range(3):
            tile = slice(m * 16, m * 16 + 16)
            left, right = h2_ref[n, tile].astype(F32), h2_ref[8 + n, tile].astype(F32)
            t_ref[pl.ds(2 * m * 128 + n, 16, stride=8), :] = jnp.where(lane16 < 64, left, right)
            if m < 2:
                t_ref[pl.ds((2 * m + 1) * 128 + n, 16, stride=8), :] = pltpu.roll(jnp.where(lane16 < 64, right, left), 64, 1)
    quarters = (0, 1, 2, 3)
    ag, ac = {}, []

    def piece(zz, half, index):
        return g_ref.at[zz, half, pl.ds(2 * index, 2)]

    def source(way, k):
        return zmod(-1 - k if way == 0 else 1 + k)

    def arrives(way, k, i):
        return k < 3 or (way == 0 and i < 2) or (way == 1 and i >= 2)

    def pass_on(way, k, i):
        zz = z if k == 0 else source(way, k - 1)
        part = piece(zz, c, quarters[i])
        copy = rdma(part, part, ag_send.at[way, k, i], ag_recv.at[way, k, i], dev(z + 1 - 2 * way, yh, c, g))
        copy.start()
        ag[(way, k, i)] = copy

    def to_core(part, other, index, k):
        copy = rdma(part, part, ac_send.at[index], ac_recv.at[index], partner)
        copy.start()
        ac.append((copy, rdma(other, other, ac_send.at[index], ac_recv.at[index], partner), k))

    def share(way, k, i):
        zz = source(way, k)
        part = piece(zz, c, quarters[i])
        to_core(part, piece(zz, 1 - c, quarters[i]), (way * 4 + k) * 4 + i, k)

    for r in range(8):
        for pair in range(STEPS // 2):
            parts = [t_ref[(2 * pair + j) * 64 + r * 8 : (2 * pair + j) * 64 + r * 8 + 8, :] for j in range(2)]
            g_ref[z, c, r, pair * 16 : pair * 16 + 16] = jnp.concatenate(parts, axis=0).astype(BF16)
        if r % 2 == 1:
            for way in range(2):
                pass_on(way, 0, r // 2)
    own_part, own_other = g_ref.at[z, c], g_ref.at[z, 1 - c]
    own_copy = rdma(own_part, own_part, ac_send.at[32], ac_recv.at[32], partner)
    own_copy.start()

    def final_arrived(i, carry):
        k = c * 8 + gmod(i)
        rdma(ffs_ref.at[pl.ds(0, 8)], ffr_ref.at[k], f_send.at[0], f_recv.at[k], partner).wait_recv()
        return carry

    lax.fori_loop(1, 8, final_arrived, 0)
    core_trials = ffr_ref.at[pl.ds(c * 8, 8)]
    finals = rdma(core_trials, core_trials, f_send.at[8], f_recv.at[16], partner)
    finals.start()
    for k in range(1, 4):
        for i in range(4):
            for way in range(2):
                if arrives(way, k, i):
                    ag[(way, k - 1, i)].wait_recv()
                    pass_on(way, k, i)
                    share(way, k - 1, i)
        for i in range(4):
            for way in range(2):
                if not arrives(way, k, i):
                    ag[(way, k - 1, i)].wait_recv()
                    share(way, k - 1, i)

    near_planes = (z, zmod(1), zmod(-1), zmod(2), zmod(-2))
    third_planes = (zmod(3), zmod(-3))
    far_planes = (zmod(4),)

    def product(region, planes):
        history = jnp.concatenate(
            [jnp.concatenate([g_ref[plane, 0, region], g_ref[plane, 1, region]], axis=0) for plane in planes], axis=1
        )
        band = jnp.concatenate(
            [band_ref[region, pl.ds(pl.multiple_of(plane * LANES, LANES), LANES), :] for plane in planes], axis=0
        )
        return jnp.dot(history, band, preferred_element_type=F32)

    def collect_near(region, carry):
        drive_ref[region] = product(region, near_planes)
        return carry

    def collect_third(region, carry):
        drive_ref[region] = drive_ref[region] + product(region, third_planes)
        return carry

    def from_core(first, last):
        for _, other, k in ac:
            if first <= k <= last:
                other.wait_recv()

    rdma(own_other, own_other, ac_send.at[32], ac_recv.at[32], partner).wait_recv()
    from_core(0, 1)
    lax.fori_loop(0, 6, collect_near, 0)
    for i in range(4):
        for way in range(2):
            if arrives(way, 3, i):
                ag[(way, 3, i)].wait_recv()
                share(way, 3, i)
    lax.fori_loop(6, 8, collect_near, 0)
    from_core(2, 2)
    lax.fori_loop(0, 8, collect_third, 0)
    other_trials = ffr_ref.at[pl.ds((1 - c) * 8, 8)]
    rdma(other_trials, other_trials, f_send.at[8], f_recv.at[16], partner).wait_recv()
    for k in range(16):
        value = pltpu.roll(ffr_ref[k], lax.rem(128 - 32 * q, 128), 1)
        ff_ref[k] = value[:, :32]

    from_core(3, 3)

    slot8 = s * slots + lax.broadcasted_iota(jnp.int32, (8, slots), 1)

    def collect(region, carry):
        drive_ref[region] = drive_ref[region] + product(region, far_planes)
        live = slot8 < live_ref[region]
        for half in range(2):
            bins = trials_of(tbins_ref, half, region)
            voltage = trials_of(tstart_ref, half, region)
            for step in range(STEPS):
                start = half * ROWS + step * 8
                voltage = 0.9 * voltage + (0.5 * SCALE) * drive_ref[region, start : start + 8, :]
                voltage = jnp.where(bins == step, -0.5, voltage)
            voltage = jnp.where(live, voltage, 0.0)
            for tile in range(8):
                tstart_ref[pl.ds(tile * 128 + half * 64 + region, 8, stride=8), :] = voltage[:, tile * LANES : tile * LANES + LANES]
        return carry

    lax.fori_loop(0, 8, collect, 0)
    for tile in range(8):
        out_ref[:, tile * LANES : tile * LANES + LANES] = tstart_ref[tile * 128 : tile * 128 + 128, :]

    for copy in cx.values():
        copy.wait_send()
    for _, copy in quad:
        copy.wait_send()
    for copy in ring.values():
        copy.wait_send()
    lax.fori_loop(1, 8, sent_all(setup_own), 0)
    for copy in near:
        copy.wait_send()
    lax.fori_loop(1, 16, sent_all(trial_own), 0)
    lax.fori_loop(0, 16, sent_all(trial_near), 0)
    lax.fori_loop(1, 16, sent_all(back), 0)
    lax.fori_loop(1, 8, sent_all(final), 0)
    finals.wait_send()
    own_copy.wait_send()
    for copy in ag.values():
        copy.wait_send()
    for copy, _, _ in ac:
        copy.wait_send()


def local(spike_bins, neuron_site, efficacy, region_live, membrane_init, field_init, rim_weights, rim_codes):
    trials, regions, slots = spike_bins.shape
    rows = trials * regions
    vmem = pl.BlockSpec(memory_space=pltpu.VMEM)
    dma = pltpu.SemaphoreType.DMA
    field_final, membranes = pl.pallas_call(
        fused_kernel,
        out_shape=(jax.ShapeDtypeStruct((trials, regions, 32), F32), jax.ShapeDtypeStruct((rows, slots), F32)),
        in_specs=[pl.BlockSpec(memory_space=pltpu.SMEM)] + [vmem] * 7,
        out_specs=(vmem, vmem),
        scratch_shapes=[
            pltpu.VMEM((regions, slots), F32),
            pltpu.VMEM((1024, LANES), jnp.int32),
            pltpu.VMEM((1024, LANES), F32),
            pltpu.VMEM((8, 1024, slots), BF16),
            pltpu.VMEM((2, 160, slots), BF16),
            pltpu.VMEM((8, 160, slots), F32),
            pltpu.VMEM((8, 2, 8, ROWS, LANES), BF16),
            pltpu.VMEM((8, 2, 8, ROWS, LANES), BF16),
            pltpu.VMEM((12, 8, LANES), F32),
            pltpu.VMEM((16, 8, LANES), F32),
            pltpu.VMEM((8, 8, ROWS, LANES), BF16),
            pltpu.VMEM((2, 4, 4, 2, ROWS, LANES), BF16),
            pltpu.VMEM((2, 4, 4, 2, ROWS, LANES), BF16),
            pltpu.VMEM((4, 12, 8, LANES), F32),
            pltpu.VMEM((4, 8, 8, LANES), F32),
            pltpu.VMEM((12, 8, LANES), F32),
            pltpu.VMEM((8, 8, LANES), F32),
            pltpu.VMEM((12, 8, LANES), F32),
            pltpu.VMEM((8, 8, LANES), F32),
            pltpu.VMEM((12, 8, LANES), F32),
            pltpu.VMEM((8, 8, LANES), F32),
            pltpu.VMEM((8, 12, 8, LANES), F32),
            pltpu.VMEM((8, 8, LANES), F32),
            pltpu.VMEM((640, LANES), F32),
            pltpu.VMEM((8, ROWS, LANES), BF16),
            pltpu.VMEM((2, 8, 32, LANES), BF16),
            pltpu.VMEM((16, ROWS, LANES), BF16),
            pltpu.VMEM((16, 32, LANES), BF16),
            pltpu.VMEM((STEPS, 64, LANES), F32),
            pltpu.VMEM((25, 64, LANES), F32),
            pltpu.VMEM((STEPS, 64, LANES), F32),
            pltpu.VMEM((8, 48, LANES), BF16),
            pltpu.VMEM((16, 48, LANES), BF16),
            pltpu.VMEM((640, LANES), F32),
            pltpu.VMEM((64, LANES), F32),
            pltpu.VMEM((16, 8, LANES), F32),
            dma((4,)), dma((4,)), dma((2, 4, 4)), dma((2, 4, 4)), dma((8,)), dma((8,)),
            dma((2,)), dma((2,)), dma((2, 8)), dma((2, 8)), dma((2, 16)), dma((2, 16)), dma((16,)), dma((16,)),
            dma((16,)), dma((17,)), dma((2, 4, 4)), dma((2, 4, 4)), dma((33,)), dma((33,)),
        ],
        compiler_params=pltpu.CompilerParams(vmem_limit_bytes=VMEM_LIMIT, collective_id=0, has_side_effects=True),
        name="window",
    )(
        region_live, spike_bins.reshape(rows, slots), neuron_site, efficacy,
        membrane_init.reshape(rows, slots), field_init, rim_weights, rim_codes,
    )
    return field_final, membranes.reshape(trials, regions, slots)


def solution(mesh):
    in_specs = (
        P(None, "neur", "surf"),
        P("neur", "surf"),
        P("neur", "surf"),
        P("neur"),
        P(None, "neur", "surf"),
        P(None, "neur", "surf"),
        P(None, "neur", "surf"),
        P(None, "neur", "surf"),
    )
    out_specs = (P(None, "neur", "surf"), P(None, "neur", "surf"))
    return jax.shard_map(local, mesh=mesh, in_specs=in_specs, out_specs=out_specs, check_vma=False)
```

```python
import math

import jax
import jax.numpy as jnp
from jax import lax
from jax.experimental import pallas as pl
from jax.experimental.pallas import tpu as pltpu
from jax.sharding import PartitionSpec as P

STEPS = 10
RIM = 2
FOOT = 8
TAPS = (0.84375, 0.51171875, 0.310546875, 0.1884765625, 0.1142578125, 0.0693359375, 0.0419921875, 0.025390625)
SCALE = 1.0 / sum(TAPS)
DECAY = math.exp(-0.35)
F32 = jnp.float32
BF16 = jnp.bfloat16
VMEM_LIMIT = 56 * 1024 * 1024
ROWS = 80
LANES = 128


def build_band(site, band_ref):
    total, slots = band_ref.shape[-2:]
    tiles = total // 16
    high = jnp.broadcast_to((site >> 4).astype(F32).astype(BF16), (16, slots))
    low = jnp.broadcast_to(site & 15, (16, slots))
    row = lax.broadcasted_iota(jnp.int32, (16, slots), 0)
    first = jnp.zeros((16, slots), F32)
    second = jnp.zeros((16, slots), F32)
    for offset in range(FOOT):
        first = jnp.where(row - low == offset, TAPS[offset], first)
        second = jnp.where(row + 16 - low == offset, TAPS[offset], second)
    first, second = first.astype(BF16), second.astype(BF16)
    zero = jnp.zeros((16, slots), BF16)
    for tile in range(tiles):
        here = high == jnp.asarray(tile, BF16)
        before = high == jnp.asarray((tile - 1) % tiles, BF16)
        band_ref[tile * 16 : tile * 16 + 16, :] = jnp.where(here, first, jnp.where(before, second, zero))


def fused_kernel(
    live_ref, bins_ref, site_ref, eff_ref, start_ref, field_ref, weights_ref, codes_ref,
    ff_ref, out_ref,
    weff_ref, tbins_ref, tstart_ref, band_ref, charge_ref, drive_ref, s_ref, g_ref, rim_ref, init_ref,
    cx_ref, sbuf, rbuf, rq_ref, iq_ref, tl_ref, til_ref, th_ref, tih_ref, tm_ref, tim_ref, ro_ref, io_ref, p_ref, mb_ref, mh_ref,
    own_ref, hal_ref, inj_ref, cf_ref, hist_ref, mb2_ref, h2_ref, t_ref, ffs_ref, ffr_ref,
    cx_send, cx_recv, ring_send, ring_recv, q_send, q_recv, n_send, n_recv, r2_send, r2_recv, a_send, a_recv,
    b_send, b_recv, f_send, f_recv, ag_send, ag_recv, ac_send, ac_recv,
):
    s = lax.axis_index("surf")
    g = lax.axis_index("neur")
    z = s // 4
    yh = (s // 2) % 2
    c = s % 2
    dzh = 2 * yh - 1

    def dev(zz, yy, cc, gg):
        return {"surf": lax.rem(zz + 16, 8) * 4 + yy * 2 + cc, "neur": gg}

    def rdma(src, dst, ss, rs, target):
        return pltpu.make_async_remote_copy(
            src_ref=src, dst_ref=dst, send_sem=ss, recv_sem=rs, device_id=target, device_id_type=pl.DeviceIdType.MESH
        )

    def zmod(dz):
        return lax.rem(z + dz + 16, 8)

    def gmod(i):
        return lax.rem(g + i, 8)

    barrier = pltpu.get_barrier_semaphore()

    def greet(target):
        pl.semaphore_signal(barrier, inc=1, device_id=target, device_id_type=pl.DeviceIdType.MESH)

    greet(dev(z, yh, 1 - c, g))
    greet(dev(z, 1 - yh, 1 - c, g))
    greet(dev(z - dzh, yh, c, g))
    for a in range(2):
        for i in range(8):
            if a or i:
                greet(dev(z, lax.rem(yh + a, 2), c, gmod(i)))
            greet(dev(z + dzh, a, c, i))

    slots = site_ref.shape[1]
    slot_id = s * slots + lax.broadcasted_iota(jnp.int32, (1, slots), 1)

    for tile in range(8):
        tbins_ref[tile * 128 : tile * 128 + 128, :] = bins_ref[:, tile * LANES : tile * LANES + LANES]
        tstart_ref[tile * 128 : tile * 128 + 128, :] = start_ref[:, tile * LANES : tile * LANES + LANES]

    weff_ref[...] = eff_ref[...].astype(F32)

    def trials_of(ref, half, region):
        first = half * 64 + region
        return jnp.concatenate([ref[pl.ds(tile * 128 + first, 8, stride=8), :] for tile in range(8)], axis=1)

    def spread(region, lot):
        weight = jnp.where(slot_id < live_ref[region], weff_ref[pl.ds(region, 1), :], 0.0)
        weight = jnp.broadcast_to(weight, (8, slots))
        band = band_ref.at[region]
        build_band(site_ref[pl.ds(region, 1), :], band)
        for half in range(2):
            bins = trials_of(tbins_ref, half, region)
            for pair in range(STEPS // 2):
                rows = [jnp.where(bins == 2 * pair + j, weight, 0.0) for j in range(2)]
                start = half * ROWS + pair * 16
                charge_ref[lot, start : start + 16, :] = jnp.concatenate(rows, axis=0).astype(BF16)
        total = lax.dot_general(charge_ref[lot], band[...], (((1,), (1,)), ((), ())), preferred_element_type=F32)
        total = (total * SCALE).astype(BF16)
        for plane in range(8):
            for half in range(2):
                s_ref[plane, half, region] = total[half * ROWS : half * ROWS + ROWS, plane * LANES : plane * LANES + LANES]

    partner = dev(z, yh, 1 - c, g)
    cx = {}

    def quarter(index):
        for lot in range(2):
            spread(2 * index + lot, lot)

    def to_partner(index):
        part = pl.ds(2 * index, 2)
        cx[index] = rdma(s_ref.at[:, 1 - c, part], cx_ref.at[:, part], cx_send.at[index], cx_recv.at[index], partner)
        cx[index].start()

    quarter(0)
    pl.semaphore_wait(barrier, 2 + 15 + 17)
    to_partner(0)

    def x_of(dz, index):
        zd = zmod(dz)
        part = slice(2 * index, 2 * index + 2)
        return s_ref[zd, c, part].astype(F32) + cx_ref[zd, part].astype(F32)

    ring = {}

    def hop(index, k):
        for way, sign in ((0, 1), (1, -1)):
            first = 4 if way == index % 2 else 3
            if k >= first:
                continue
            value = x_of(sign * (first - k), index)
            if k == 0:
                pass
            else:
                ring[(way, index, k - 1)].wait_recv()
                value = value + rbuf[way, index, k - 1].astype(F32)
            sbuf[way, index, k] = value.astype(BF16)
            copy = rdma(
                sbuf.at[way, index, k], rbuf.at[way, index, k], ring_send.at[way, index, k], ring_recv.at[way, index, k],
                dev(z + sign, yh, c, g),
            )
            copy.start()
            ring[(way, index, k)] = copy

    quarter(1)
    to_partner(1)
    cx[0].wait_recv()
    hop(0, 0)
    q = yh * 2 + c
    for k in range(6):
        rim_ref[k] = jnp.concatenate([weights_ref[k]] * 4, axis=1)
        rim_ref[6 + k] = jnp.concatenate([codes_ref[k].astype(F32)] * 4, axis=1)
    for k in range(16):
        init_ref[k] = jnp.concatenate([field_ref[k]] * 4, axis=1)
    quad = []
    for i in range(1, 4):
        y2 = lax.rem(yh + i // 2, 2)
        c2 = lax.rem(c + i % 2, 2)
        target = dev(z, y2, c2, g)
        quad.append((y2 * 2 + c2, rdma(rim_ref, rq_ref.at[q], q_send.at[i], q_recv.at[q], target)))
        quad.append((y2 * 2 + c2, rdma(init_ref.at[pl.ds(c2 * 8, 8)], iq_ref.at[q], q_send.at[4 + i], q_recv.at[4 + q], target)))
    for _, copy in quad:
        copy.start()
    rq_ref[q] = rim_ref[...]
    iq_ref[q] = init_ref[pl.ds(c * 8, 8)]


    quarter(2)
    to_partner(2)
    cx[1].wait_recv()
    hop(1, 0)
    hop(0, 1)
    quarter(3)
    to_partner(3)
    cx[2].wait_recv()
    hop(2, 0)
    hop(1, 1)
    hop(0, 2)

    lane = lax.broadcasted_iota(jnp.int32, (8, LANES), 1)
    for i in range(1, 4):
        y2 = lax.rem(yh + i // 2, 2)
        c2 = lax.rem(c + i % 2, 2)
        src = y2 * 2 + c2
        rdma(rim_ref, rq_ref.at[src], q_send.at[i], q_recv.at[src], partner).wait_recv()
        rdma(init_ref.at[pl.ds(0, 8)], iq_ref.at[src], q_send.at[4 + i], q_recv.at[4 + src], partner).wait_recv()
    block = lane // 32
    for k in range(12):
        tl_ref[k] = jnp.where(
            block < 2,
            jnp.where(block == 0, rq_ref[0, k], rq_ref[1, k]),
            jnp.where(block == 2, rq_ref[2, k], rq_ref[3, k]),
        )
    for k in range(8):
        til_ref[k] = jnp.where(
            block < 2,
            jnp.where(block == 0, iq_ref[0, k], iq_ref[1, k]),
            jnp.where(block == 2, iq_ref[2, k], iq_ref[3, k]),
        )

    near = (
        rdma(tl_ref, th_ref, n_send.at[0], n_recv.at[0], dev(z - dzh, yh, c, g)),
        rdma(til_ref, tih_ref, n_send.at[1], n_recv.at[1], dev(z - dzh, yh, c, g)),
    )
    for copy in near:
        copy.start()

    def setup_own(i):
        gg = gmod(i)
        target = dev(z, yh, c, gg)
        return (
            rdma(tm_ref, ro_ref.at[g], r2_send.at[0, i], r2_recv.at[0, g], target),
            rdma(tim_ref.at[gg], io_ref.at[g], r2_send.at[1, i], r2_recv.at[1, g], target),
        )

    def start_all(make):
        def body(i, carry):
            for copy in make(i):
                copy.start()
            return carry

        return body

    def sent_all(make):
        def body(i, carry):
            for copy in make(i):
                copy.wait_send()
            return carry

        return body

    cx[3].wait_recv()
    hop(3, 0)
    hop(2, 1)
    hop(1, 2)

    mine = (lane >= 32 * yh) & (lane < 96 + 32 * yh)
    for copy in near:
        copy.wait_recv()
    for k in range(12):
        tm_ref[k] = jnp.where(mine, tl_ref[k], th_ref[k])
    for k in range(8):
        tim_ref[k] = jnp.where(mine, til_ref[k], tih_ref[k])
    lax.fori_loop(1, 8, start_all(setup_own), 0)
    ro_ref[g] = tm_ref[...]
    io_ref[g] = tim_ref[g]

    hop(0, 3)
    hop(3, 1)
    hop(2, 2)

    hop(1, 3)
    hop(3, 2)
    hop(2, 3)
    hop(3, 3)

    def setup_arrived(i, carry):
        gg = gmod(i)
        rdma(tm_ref, ro_ref.at[gg], r2_send.at[0, i], r2_recv.at[0, gg], partner).wait_recv()
        rdma(tim_ref.at[0], io_ref.at[gg], r2_send.at[1, i], r2_recv.at[1, gg], partner).wait_recv()
        return carry

    lax.fori_loop(1, 8, setup_arrived, 0)
    row8 = lax.broadcasted_iota(jnp.int32, (8, LANES), 0)

    def couple(gg, carry):
        weights = [ro_ref[gg, k] for k in range(6)]
        codes = [ro_ref[gg, 6 + k] for k in range(6)]
        rows = pl.ds(pl.multiple_of(gg * 8, 8), 8)
        region = gg * 8 + row8
        for a in range(-RIM, RIM + 1):
            inside = (region + a >= 0) & (region + a < 64)
            for b in range(-RIM, RIM + 1):
                code = (a + RIM) * (2 * RIM + 1) + b + RIM
                if a == 0 and b == 0:
                    cf_ref[code, rows] = 0.9 - 0.15 * (weights[0] + weights[1] + weights[2] + weights[3] + weights[4] + weights[5])
                    continue
                total = jnp.zeros((8, LANES), F32)
                for k in range(6):
                    total = total + jnp.where(codes[k] == float(code), weights[k], 0.0)
                cf_ref[code, rows] = jnp.where(inside, 0.15 * total, 0.0)
        ffs_ref[rows] = io_ref[gg]
        return carry

    lax.fori_loop(0, 8, couple, 0)
    for a in range(-RIM, RIM + 1):
        if a != 0:
            for b in range(2 * RIM + 1):
                code = (a + RIM) * (2 * RIM + 1) + b
                cf_ref[code] = pltpu.roll(cf_ref[code], a % 64, 0)

    for index in range(4):
        value = x_of(0, index)
        for way in range(2):
            k = 3 if way == index % 2 else 2
            ring[(way, index, k)].wait_recv()
            value = value + rbuf[way, index, k].astype(F32)
        p_ref[index * 160 : index * 160 + 160, :] = value.reshape(160, LANES)

    lane16 = lax.broadcasted_iota(jnp.int32, (16, LANES), 1)
    block16 = lane16 // 32

    def by_block(tiles):
        return jnp.where(
            block16 < 2, jnp.where(block16 == 0, tiles[0], tiles[1]), jnp.where(block16 == 2, tiles[2], tiles[3])
        )

    slot = yh * 8 + g

    def trial_own(k):
        n = gmod(k % 8)
        return (rdma(mb_ref.at[n], own_ref.at[slot], a_send.at[0, k], a_recv.at[0, slot], dev(z, lax.rem(yh + k // 8, 2), c, n)),)

    def trial_near(k):
        n = gmod(k % 8)
        up = k // 8
        return (rdma(mh_ref.at[up, n], hal_ref.at[slot], a_send.at[1, k], a_recv.at[1, slot], dev(z + 1 - 2 * up, up, c, n)),)

    def trial_send(i, carry):
        n = gmod(i)
        tiles = []
        for pair in range(STEPS // 2):
            parts = [p_ref[pl.ds((2 * pair + j) * 8 + n, 8, stride=ROWS), :] for j in range(2)]
            tiles.append(jnp.concatenate(parts, axis=0))
            mb_ref[n, pair * 16 : pair * 16 + 16] = tiles[-1].astype(BF16)
        high = [pltpu.roll(tiles[j], 32 * j + 32, 1) if j < 3 else tiles[j] for j in range(4)]
        low = [pltpu.roll(tiles[j], 32 * j, 1) if j > 0 else tiles[j] for j in range(4)]
        mh_ref[0, n, :16] = by_block(high).astype(BF16)
        mh_ref[1, n, :16] = by_block(low).astype(BF16)
        mh_ref[0, n, 16:] = tiles[4].astype(BF16)
        mh_ref[1, n, 16:] = tiles[4].astype(BF16)
        trial_own(i + 8)[0].start()
        trial_near(i)[0].start()
        trial_near(i + 8)[0].start()

        @pl.when(i > 0)
        def _():
            trial_own(i)[0].start()

        return carry

    lax.fori_loop(1, 8, trial_send, 0)
    trial_send(0, 0)
    own_ref[slot] = mb_ref[g]

    def trial_arrived(k, carry):
        @pl.when(k != slot)
        def _():
            rdma(mb_ref.at[0], own_ref.at[k], a_send.at[0, 0], a_recv.at[0, k], partner).wait_recv()

        rdma(mh_ref.at[0, 0], hal_ref.at[k], a_send.at[1, 0], a_recv.at[1, k], partner).wait_recv()
        return carry

    lax.fori_loop(0, 16, trial_arrived, 0)
    mine16 = (lane16 >= 32 * yh) & (lane16 < 96 + 32 * yh)

    def unpack(gg, carry):
        rows = pl.ds(pl.multiple_of(gg * 8, 8), 8)
        edge = hal_ref[gg].astype(F32) + hal_ref[8 + gg].astype(F32)
        for pair in range(STEPS // 2):
            tile = slice(pair * 16, pair * 16 + 16)
            near_edge = pltpu.roll(edge[:16], lax.rem(96 * (1 - yh) - 32 * pair + 128, 128), 1) if pair < 4 else edge[16:]
            value = jnp.where(mine16, own_ref[gg, tile].astype(F32) + own_ref[8 + gg, tile].astype(F32), near_edge)
            inj_ref[2 * pair, rows] = value[:8]
            inj_ref[2 * pair + 1, rows] = value[8:]
        return carry

    lax.fori_loop(0, 8, unpack, 0)

    def advance(step, carry):
        field, rate = carry
        rate = DECAY * rate + inj_ref[step]
        total = 0.1 * rate
        shifted = [field if b == 0 else pltpu.roll(field, (-b) % LANES, 1) for b in range(-RIM, RIM + 1)]
        for a in range(-RIM, RIM + 1):
            term = None
            for b in range(2 * RIM + 1):
                product = cf_ref[(a + RIM) * (2 * RIM + 1) + b] * shifted[b]
                term = product if term is None else term + product
            total = total + (term if a == 0 else pltpu.roll(term, (-a) % 64, 0))
        hist_ref[step] = total
        return (total, rate)

    last, _ = lax.fori_loop(0, STEPS, advance, (ffs_ref[...], jnp.zeros((64, LANES), F32)))
    ffs_ref[...] = last

    mine64 = (lane16 >= 64 * yh) & (lane16 < 64 + 64 * yh)

    trial = c * 8 + g

    def back(k):
        gg = gmod(k % 8)
        return (rdma(mb2_ref.at[gg], h2_ref.at[slot], b_send.at[k], b_recv.at[slot], dev(z, lax.rem(yh + k // 8, 2), c, gg)),)

    def final(k):
        gg = gmod(k % 8)
        rows = pl.ds(pl.multiple_of(gg * 8, 8), 8)
        return (rdma(ffs_ref.at[rows], ffr_ref.at[trial], f_send.at[k], f_recv.at[trial], dev(z, yh, c, gg)),)

    def pack(i, carry):
        gg = gmod(i)
        rows = pl.ds(pl.multiple_of(gg * 8, 8), 8)
        tiles = [
            jnp.concatenate([hist_ref[2 * pair, rows], hist_ref[2 * pair + 1, rows]], axis=0) for pair in range(STEPS // 2)
        ]
        for m in range(2):
            both = jnp.where(mine64, tiles[2 * m], pltpu.roll(tiles[2 * m + 1], 64, 1))
            mb2_ref[gg, m * 16 : m * 16 + 16] = both.astype(BF16)
        mb2_ref[gg, 32:48] = tiles[4].astype(BF16)
        back(i + 8)[0].start()

        @pl.when(i > 0)
        def _():
            back(i)[0].start()

        return carry

    lax.fori_loop(1, 8, pack, 0)
    pack(0, 0)
    lax.fori_loop(1, 8, start_all(final), 0)
    h2_ref[slot] = mb2_ref[g]
    ffr_ref[trial] = ffs_ref[pl.ds(pl.multiple_of(g * 8, 8), 8)]

    def back_arrived(k, carry):
        @pl.when(k != slot)
        def _():
            rdma(mb2_ref.at[0], h2_ref.at[k], b_send.at[0], b_recv.at[k], partner).wait_recv()

        return carry

    lax.fori_loop(0, 16, back_arrived, 0)
    for n in range(8):
        for m in range(3):
            tile = slice(m * 16, m * 16 + 16)
            left, right = h2_ref[n, tile].astype(F32), h2_ref[8 + n, tile].astype(F32)
            t_ref[pl.ds(2 * m * 128 + n, 16, stride=8), :] = jnp.where(lane16 < 64, left, right)
            if m < 2:
                t_ref[pl.ds((2 * m + 1) * 128 + n, 16, stride=8), :] = pltpu.roll(jnp.where(lane16 < 64, right, left), 64, 1)
    quarters = (0, 1, 2, 3)
    ag, ac = {}, []

    def piece(zz, half, index):
        return g_ref.at[zz, half, pl.ds(2 * index, 2)]

    def source(way, k):
        return zmod(-1 - k if way == 0 else 1 + k)

    def arrives(way, k, i):
        return k < 3 or (way == 0 and i < 2) or (way == 1 and i >= 2)

    def pass_on(way, k, i):
        zz = z if k == 0 else source(way, k - 1)
        part = piece(zz, c, quarters[i])
        copy = rdma(part, part, ag_send.at[way, k, i], ag_recv.at[way, k, i], dev(z + 1 - 2 * way, yh, c, g))
        copy.start()
        ag[(way, k, i)] = copy

    def to_core(part, other, index, k):
        copy = rdma(part, part, ac_send.at[index], ac_recv.at[index], partner)
        copy.start()
        ac.append((copy, rdma(other, other, ac_send.at[index], ac_recv.at[index], partner), k))

    def share(way, k, i):
        zz = source(way, k)
        part = piece(zz, c, quarters[i])
        to_core(part, piece(zz, 1 - c, quarters[i]), (way * 4 + k) * 4 + i, k)

    for r in range(8):
        for pair in range(STEPS // 2):
            parts = [t_ref[(2 * pair + j) * 64 + r * 8 : (2 * pair + j) * 64 + r * 8 + 8, :] for j in range(2)]
            g_ref[z, c, r, pair * 16 : pair * 16 + 16] = jnp.concatenate(parts, axis=0).astype(BF16)
        if r % 2 == 1:
            for way in range(2):
                pass_on(way, 0, r // 2)
    own_part, own_other = g_ref.at[z, c], g_ref.at[z, 1 - c]
    own_copy = rdma(own_part, own_part, ac_send.at[32], ac_recv.at[32], partner)
    own_copy.start()

    def final_arrived(i, carry):
        k = c * 8 + gmod(i)
        rdma(ffs_ref.at[pl.ds(0, 8)], ffr_ref.at[k], f_send.at[0], f_recv.at[k], partner).wait_recv()
        return carry

    lax.fori_loop(1, 8, final_arrived, 0)
    core_trials = ffr_ref.at[pl.ds(c * 8, 8)]
    finals = rdma(core_trials, core_trials, f_send.at[8], f_recv.at[16], partner)
    finals.start()
    for k in range(1, 4):
        for i in range(4):
            for way in range(2):
                if arrives(way, k, i):
                    ag[(way, k - 1, i)].wait_recv()
                    pass_on(way, k, i)
                    share(way, k - 1, i)
        for i in range(4):
            for way in range(2):
                if not arrives(way, k, i):
                    ag[(way, k - 1, i)].wait_recv()
                    share(way, k - 1, i)

    near_planes = (z, zmod(1), zmod(-1), zmod(2), zmod(-2))
    third_planes = (zmod(3), zmod(-3))
    far_planes = (zmod(4),)

    def product(region, planes):
        history = jnp.concatenate(
            [jnp.concatenate([g_ref[plane, 0, region], g_ref[plane, 1, region]], axis=0) for plane in planes], axis=1
        )
        band = jnp.concatenate(
            [band_ref[region, pl.ds(pl.multiple_of(plane * LANES, LANES), LANES), :] for plane in planes], axis=0
        )
        return jnp.dot(history, band, preferred_element_type=F32)

    def collect_near(region, carry):
        drive_ref[region] = product(region, near_planes)
        return carry

    def collect_third(region, carry):
        drive_ref[region] = drive_ref[region] + product(region, third_planes)
        return carry

    def from_core(first, last):
        for _, other, k in ac:
            if first <= k <= last:
                other.wait_recv()

    rdma(own_other, own_other, ac_send.at[32], ac_recv.at[32], partner).wait_recv()
    from_core(0, 1)
    lax.fori_loop(0, 6, collect_near, 0)
    for i in range(4):
        for way in range(2):
            if arrives(way, 3, i):
                ag[(way, 3, i)].wait_recv()
                share(way, 3, i)
    lax.fori_loop(6, 8, collect_near, 0)
    from_core(2, 2)
    lax.fori_loop(0, 8, collect_third, 0)
    other_trials = ffr_ref.at[pl.ds((1 - c) * 8, 8)]
    rdma(other_trials, other_trials, f_send.at[8], f_recv.at[16], partner).wait_recv()
    for k in range(16):
        value = pltpu.roll(ffr_ref[k], lax.rem(128 - 32 * q, 128), 1)
        ff_ref[k] = value[:, :32]

    from_core(3, 3)

    slot8 = s * slots + lax.broadcasted_iota(jnp.int32, (8, slots), 1)

    def collect(region, carry):
        drive_ref[region] = drive_ref[region] + product(region, far_planes)
        live = slot8 < live_ref[region]
        for half in range(2):
            bins = trials_of(tbins_ref, half, region)
            voltage = trials_of(tstart_ref, half, region)
            for step in range(STEPS):
                start = half * ROWS + step * 8
                voltage = 0.9 * voltage + (0.5 * SCALE) * drive_ref[region, start : start + 8, :]
                voltage = jnp.where(bins == step, -0.5, voltage)
            voltage = jnp.where(live, voltage, 0.0)
            for tile in range(8):
                tstart_ref[pl.ds(tile * 128 + half * 64 + region, 8, stride=8), :] = voltage[:, tile * LANES : tile * LANES + LANES]
        return carry

    lax.fori_loop(0, 8, collect, 0)
    for tile in range(8):
        out_ref[:, tile * LANES : tile * LANES + LANES] = tstart_ref[tile * 128 : tile * 128 + 128, :]

    for copy in cx.values():
        copy.wait_send()
    for _, copy in quad:
        copy.wait_send()
    for copy in ring.values():
        copy.wait_send()
    lax.fori_loop(1, 8, sent_all(setup_own), 0)
    for copy in near:
        copy.wait_send()
    lax.fori_loop(1, 16, sent_all(trial_own), 0)
    lax.fori_loop(0, 16, sent_all(trial_near), 0)
    lax.fori_loop(1, 16, sent_all(back), 0)
    lax.fori_loop(1, 8, sent_all(final), 0)
    finals.wait_send()
    own_copy.wait_send()
    for copy in ag.values():
        copy.wait_send()
    for copy, _, _ in ac:
        copy.wait_send()


def local(spike_bins, neuron_site, efficacy, region_live, membrane_init, field_init, rim_weights, rim_codes):
    trials, regions, slots = spike_bins.shape
    rows = trials * regions
    vmem = pl.BlockSpec(memory_space=pltpu.VMEM)
    dma = pltpu.SemaphoreType.DMA
    field_final, membranes = pl.pallas_call(
        fused_kernel,
        out_shape=(jax.ShapeDtypeStruct((trials, regions, 32), F32), jax.ShapeDtypeStruct((rows, slots), F32)),
        in_specs=[pl.BlockSpec(memory_space=pltpu.SMEM)] + [vmem] * 7,
        out_specs=(vmem, vmem),
        scratch_shapes=[
            pltpu.VMEM((regions, slots), F32),
            pltpu.VMEM((1024, LANES), jnp.int32),
            pltpu.VMEM((1024, LANES), F32),
            pltpu.VMEM((8, 1024, slots), BF16),
            pltpu.VMEM((2, 160, slots), BF16),
            pltpu.VMEM((8, 160, slots), F32),
            pltpu.VMEM((8, 2, 8, ROWS, LANES), BF16),
            pltpu.VMEM((8, 2, 8, ROWS, LANES), BF16),
            pltpu.VMEM((12, 8, LANES), F32),
            pltpu.VMEM((16, 8, LANES), F32),
            pltpu.VMEM((8, 8, ROWS, LANES), BF16),
            pltpu.VMEM((2, 4, 4, 2, ROWS, LANES), BF16),
            pltpu.VMEM((2, 4, 4, 2, ROWS, LANES), BF16),
            pltpu.VMEM((4, 12, 8, LANES), F32),
            pltpu.VMEM((4, 8, 8, LANES), F32),
            pltpu.VMEM((12, 8, LANES), F32),
            pltpu.VMEM((8, 8, LANES), F32),
            pltpu.VMEM((12, 8, LANES), F32),
            pltpu.VMEM((8, 8, LANES), F32),
            pltpu.VMEM((12, 8, LANES), F32),
            pltpu.VMEM((8, 8, LANES), F32),
            pltpu.VMEM((8, 12, 8, LANES), F32),
            pltpu.VMEM((8, 8, LANES), F32),
            pltpu.VMEM((640, LANES), F32),
            pltpu.VMEM((8, ROWS, LANES), BF16),
            pltpu.VMEM((2, 8, 32, LANES), BF16),
            pltpu.VMEM((16, ROWS, LANES), BF16),
            pltpu.VMEM((16, 32, LANES), BF16),
            pltpu.VMEM((STEPS, 64, LANES), F32),
            pltpu.VMEM((25, 64, LANES), F32),
            pltpu.VMEM((STEPS, 64, LANES), F32),
            pltpu.VMEM((8, 48, LANES), BF16),
            pltpu.VMEM((16, 48, LANES), BF16),
            pltpu.VMEM((640, LANES), F32),
            pltpu.VMEM((64, LANES), F32),
            pltpu.VMEM((16, 8, LANES), F32),
            dma((4,)), dma((4,)), dma((2, 4, 4)), dma((2, 4, 4)), dma((8,)), dma((8,)),
            dma((2,)), dma((2,)), dma((2, 8)), dma((2, 8)), dma((2, 16)), dma((2, 16)), dma((16,)), dma((16,)),
            dma((16,)), dma((17,)), dma((2, 4, 4)), dma((2, 4, 4)), dma((33,)), dma((33,)),
        ],
        compiler_params=pltpu.CompilerParams(vmem_limit_bytes=VMEM_LIMIT, collective_id=0, has_side_effects=True),
        name="window",
    )(
        region_live, spike_bins.reshape(rows, slots), neuron_site, efficacy,
        membrane_init.reshape(rows, slots), field_init, rim_weights, rim_codes,
    )
    return field_final, membranes.reshape(trials, regions, slots)


def solution(mesh):
    in_specs = (
        P(None, "neur", "surf"),
        P("neur", "surf"),
        P("neur", "surf"),
        P("neur"),
        P(None, "neur", "surf"),
        P(None, "neur", "surf"),
        P(None, "neur", "surf"),
        P(None, "neur", "surf"),
    )
    out_specs = (P(None, "neur", "surf"), P(None, "neur", "surf"))
    return jax.shard_map(local, mesh=mesh, in_specs=in_specs, out_specs=out_specs, check_vma=False)
```
